256 devices in a mesh: pair: 32 (over x, y, core), edge: 8 (over z).
Axes of the slice: x: 4, y: 4, z: 8, core: 2. Of those that a mesh axis runs over, the one named last changes fastest.
Arguments:
- entities: bfloat16 [64, 2048, 200], P(None, ('pair', 'edge')), may hold values from -5.1 to 5.1
- relations: float32 [4131, 200], replicated, may hold values from -1.5 to 1.5
- edge_src: int32 [32, 32768], P('pair', 'edge'), may hold values from 0 to 2047
- edge_rel: int32 [32, 32768], P('pair', 'edge'), may hold values from 0 to 4130
- edge_dst: int32 [32, 32768], P('pair', 'edge'), may hold values from 0 to 2047
- negatives: int32 [32, 64, 1024], P('pair', 'edge'), may hold values from 0 to 2047
- pair_live: int32 [32], P('pair'), may hold values from 1 to 32768, 524288 in all
- pair_plan: int32 [32, 2], replicated, may hold values from 0 to 63, as said below
Outputs:
- ent_grad: float32 [64, 2048, 200], P(None, ('pair', 'edge'))
- rel_grad: float32 [4131, 200], replicated
The draws below stay inside these ranges and needn't reach their ends.
Inputs may be any that keep to these rules, and one draw needn't show every extreme that they name: `pair_plan`: each of the 64 partitions appears exactly once in the plan. `pair_live`: one pair has all 32768 slots live.
All inputs are finite; a program needn't handle non-finite values. No bound on the sum of `pair_live` on one device may be relied on, other than what follows from the above.
Results may differ from the reference program's by a relative error of at most 0.00065.
The reference program's roundings to bfloat16 on the way (of `query` and `weights_b`) count: a program that leaves them out, or rounds other values in their place, can miss the bound.
Values may be sent and summed in bfloat16 or wider, within the bound.
A program may use at most 128 MiB of HBM per device.

```python
import math
import jax
import jax.numpy as jnp
import numpy as np
from jax import lax

DIM = 200
NREL = 4131
SPAN = 512
NEG = 1024
SPANS_DEV = 8
EDGES_PAIR = 32768
PARTS_SIZE = 64
ENT_BLK = 2048
N_PAIR = 32
N_EDGE = 8


def draw_entities(key, part):
    key = jax.random.fold_in(key, 11)
    scale_key, value_key = jax.random.split(key, 2)
    shape = (PARTS_SIZE, ENT_BLK, DIM)
    row_scale = jnp.exp(jax.random.uniform(scale_key, (PARTS_SIZE, ENT_BLK, 1), jnp.float32, math.log(0.1), math.log(0.5)))
    values = jnp.clip(jax.random.normal(value_key, shape, jnp.float32), -5.0, 5.0)
    return (values * row_scale).astype(jnp.bfloat16)


def draw_pair_plan(key, part):
    key = jax.random.fold_in(key, 23)
    return jax.random.permutation(key, 2 * N_PAIR).astype(jnp.int32).reshape(N_PAIR, 2)


def touch_ends(array, own_key, smallest, largest):
    shape = array.shape
    place = [jax.random.randint(jax.random.fold_in(own_key, axis), (), 0, shape[axis]) for axis in range(len(shape))]
    array = array.at[tuple(place)].set(smallest)
    longest = shape.index(max(shape))
    place[longest] = (place[longest] + 1) % shape[longest]
    return array.at[tuple(place)].set(largest)


def profile(amount, total, reach, slope):
    weights = [(1 << 20) // math.isqrt(grade ** slope) + 1 for grade in range(2, amount + 1)]
    spare, holding = total - reach - (amount - 1), [1] * (amount - 1)
    while spare > 0:
        movable = [i for i in range(amount - 1) if holding[i] < reach]
        whole, budget = sum([weights[i] for i in movable]), spare
        for i in movable:
            extra = min(reach - holding[i], max(1, budget * weights[i] // whole), spare)
            holding[i] = holding[i] + extra
            spare = spare - extra
    return np.array([reach] + holding)


def ragged(rng, number_of, total, bound, skew):
    if number_of == 2:
        one = jax.random.randint(rng, (), max(1, total - bound), min(bound, total - 1) + 1)
        return jnp.stack([one, total - one])
    lengths = jnp.asarray(profile(number_of, total, bound, skew), jnp.int32)
    twos = (number_of - 1) // 2
    donor, taker = lengths[1:1 + 2 * twos:2], lengths[2:2 + 2 * twos:2]
    slack = jnp.minimum(donor - 1, bound - taker)
    moved = jax.random.randint(jax.random.fold_in(rng, 1), (twos,), 0, 1 << 20) % (slack + 1)
    lengths = lengths.at[1:1 + 2 * twos:2].set(donor - moved).at[2:2 + 2 * twos:2].set(taker + moved)
    return lengths[jax.random.permutation(jax.random.fold_in(rng, 2), number_of)]


def setup_inputs(seed: int = 0) -> dict:
    key_list = jax.random.split(jax.random.key(seed), 9)
    entities = draw_entities(jax.random.fold_in(key_list[8], 71), 0)
    relations = jnp.clip(jax.random.uniform(key_list[1], (NREL, DIM), jnp.float32, -1.5, 1.5), -1.5, 1.5)
    edge_src = touch_ends(jax.random.randint(key_list[2], (N_PAIR, EDGES_PAIR), 0, ENT_BLK), jax.random.fold_in(key_list[2], 1), 0, ENT_BLK - 1).astype(jnp.int32)
    edge_rel = touch_ends(jax.random.randint(key_list[3], (N_PAIR, EDGES_PAIR), 0, NREL), jax.random.fold_in(key_list[3], 1), 0, NREL - 1).astype(jnp.int32)
    edge_dst = touch_ends(jax.random.randint(key_list[4], (N_PAIR, EDGES_PAIR), 0, ENT_BLK), jax.random.fold_in(key_list[4], 1), 0, ENT_BLK - 1).astype(jnp.int32)
    negatives = touch_ends(jax.random.randint(key_list[5], (N_PAIR, N_EDGE * SPANS_DEV, NEG), 0, ENT_BLK), jax.random.fold_in(key_list[5], 1), 0, ENT_BLK - 1).astype(jnp.int32)
    pair_live = ragged(key_list[6], N_PAIR, EDGES_PAIR * N_PAIR // 2, EDGES_PAIR, 2).astype(jnp.int32)
    pair_plan = draw_pair_plan(jax.random.fold_in(key_list[8], 71), 0)
    return dict(entities=entities, relations=relations, edge_src=edge_src, edge_rel=edge_rel, edge_dst=edge_dst, negatives=negatives, pair_live=pair_live, pair_plan=pair_plan)


def span_grads(source_block, target_block, relations, src_ids, rel_ids, dst_ids, neg_ids, start, live_count):
    half = relations.shape[1] // 2
    source = source_block[src_ids].astype(jnp.float32)
    target = target_block[dst_ids]
    relation = relations[rel_ids]
    src_re, src_im = source[:, :half], source[:, half:]
    rel_re, rel_im = relation[:, :half], relation[:, half:]
    query = jnp.concatenate([src_re * rel_re - src_im * rel_im, src_re * rel_im + src_im * rel_re], axis=1).astype(jnp.bfloat16)
    negative = target_block[neg_ids]
    positive = jnp.sum(query.astype(jnp.float32) * target.astype(jnp.float32), axis=1)
    scores = jnp.dot(query, negative.T, preferred_element_type=jnp.float32)
    peak = jnp.maximum(positive, jnp.max(scores, axis=1))
    pos_exp = jnp.exp(positive - peak)
    neg_exp = jnp.exp(scores - peak[:, None])
    denominator = pos_exp + jnp.sum(neg_exp, axis=1)
    live_mask = ((start + jnp.arange(src_ids.shape[0], dtype=jnp.int32)) < live_count).astype(jnp.float32)
    pos_coef = (pos_exp / denominator - 1.0) * live_mask
    weights_b = (neg_exp / denominator[:, None] * live_mask[:, None]).astype(jnp.bfloat16)
    grad_query = pos_coef[:, None] * target.astype(jnp.float32) + jnp.dot(weights_b, negative, preferred_element_type=jnp.float32)
    grad_neg = jnp.dot(weights_b.T, query, preferred_element_type=jnp.float32)
    grad_pos = pos_coef[:, None] * query.astype(jnp.float32)
    grad_re, grad_im = grad_query[:, :half], grad_query[:, half:]
    grad_source = jnp.concatenate([grad_re * rel_re + grad_im * rel_im, grad_im * rel_re - grad_re * rel_im], axis=1)
    grad_relation = jnp.concatenate([grad_re * src_re + grad_im * src_im, grad_im * src_re - grad_re * src_im], axis=1)
    return grad_source, grad_pos, grad_neg, grad_relation


def reference(entities, relations, edge_src, edge_rel, edge_dst, negatives, pair_live, pair_plan):
    blocks_pair = N_EDGE * SPANS_DEV
    starts = jnp.arange(blocks_pair, dtype=jnp.int32) * SPAN

    def per_pair(rel_total, inputs):
        src_all, rel_all, dst_all, neg_all, live_count, plan_row = inputs
        source_block = entities[plan_row[0]]
        target_block = entities[plan_row[1]]

        def per_block(carry, items):
            src_grad, dst_grad, rel_grad = carry
            src_ids, rel_ids, dst_ids, neg_ids, start = items
            grad_source, grad_pos, grad_neg, grad_relation = span_grads(source_block, target_block, relations, src_ids, rel_ids, dst_ids, neg_ids, start, live_count)
            src_grad = src_grad.at[src_ids].add(grad_source)
            dst_grad = dst_grad.at[dst_ids].add(grad_pos).at[neg_ids].add(grad_neg)
            rel_grad = rel_grad.at[rel_ids].add(grad_relation)
            return (src_grad, dst_grad, rel_grad), None

        empty = jnp.zeros((ENT_BLK, DIM), jnp.float32)
        (src_grad, dst_grad, rel_total), unused = lax.scan(per_block, (empty, empty, rel_total), (src_all.reshape(blocks_pair, SPAN), rel_all.reshape(blocks_pair, SPAN), dst_all.reshape(blocks_pair, SPAN), neg_all, starts))
        return rel_total, jnp.stack([src_grad, dst_grad])

    rel_grad, block_grads = lax.scan(per_pair, jnp.zeros((NREL, DIM), jnp.float32), (edge_src, edge_rel, edge_dst, negatives, pair_live, pair_plan))
    ent_grad = jnp.zeros((PARTS_SIZE, ENT_BLK, DIM), jnp.float32).at[pair_plan.reshape(-1)].set(block_grads.reshape(2 * N_PAIR, ENT_BLK, DIM))
    return ent_grad, rel_grad
```

```python
import functools
import jax
import jax.numpy as jnp
from jax import lax
from jax.experimental import pallas as pl
from jax.experimental.pallas import tpu as pltpu
from jax.sharding import PartitionSpec as P

DIM = 200
HALF = 100
HPAD = 104
FEAT = 208
NREL = 4131
RTILE = 256
RTILES = 17
SPAN = 512
SPANS_DEV = 8
SLOTS = SPAN * SPANS_DEV
ROWS = 2048
CHUNK = 256
NN = (((1,), (0,)), ((), ()))
NT = (((1,), (1,)), ((), ()))


def mm(a, b, dims=NN):
    return lax.dot_general(a, b, dims, preferred_element_type=jnp.float32)


def split2(v):
    hi = v.astype(jnp.bfloat16)
    lo = (v - hi.astype(jnp.float32)).astype(jnp.bfloat16)
    return jnp.concatenate([hi, lo], axis=0)


def edge_kernel(
    meta_ref, relid_ref, pos_ref, tile_ref,
    src_ref, dst_ref, neg_ref, relf_ref, s_ref, t_ref, table_ref,
    ent_ref, rel_ref,
    tn_ref, sc_ref, w_ref, ohs_ref, ohd_ref, ct_ref, rows_ref, perm_ref, sort_ref,
):
    live_blocks = meta_ref[0]
    live_here = meta_ref[1]
    ent_ref[...] = jnp.zeros_like(ent_ref)
    for h in range(ROWS // CHUNK):
        part = t_ref[:, h * CHUNK:(h + 1) * CHUNK].astype(jnp.float32)
        part = jnp.concatenate([part, jnp.zeros((256 - FEAT, CHUNK), jnp.float32)], axis=0)
        tn_ref[h * CHUNK:(h + 1) * CHUNK, :] = part.T.astype(jnp.bfloat16)

    def block(b, carry):
        def fetch_row(j, c):
            rows_ref[j] = table_ref[relid_ref[b * SPAN + j]]
            return c

        lax.fori_loop(0, SPAN, fetch_row, 0, unroll=16)
        src_row = src_ref[b]
        dst_row = dst_ref[b]
        neg_row = neg_ref[b]
        for h in range(ROWS // CHUNK):
            ids = lax.broadcasted_iota(jnp.int32, (CHUNK, SPAN), 0) + h * CHUNK
            at = pl.ds(h * CHUNK, CHUNK)
            ohs_ref[at, :] = jnp.where(ids == src_row, 1.0, 0.0).astype(jnp.bfloat16)
            ohd_ref[at, :] = jnp.where(ids == dst_row, 1.0, 0.0).astype(jnp.bfloat16)
        neg_hi = neg_row // 128
        neg_lo = neg_row - neg_hi * 128
        oh_hi = jnp.where(lax.broadcasted_iota(jnp.int32, (16, 1024), 0) == neg_hi, 1.0, 0.0).astype(jnp.bfloat16)
        oh_lo = jnp.where(lax.broadcasted_iota(jnp.int32, (128, 1024), 0) == neg_lo, 1.0, 0.0).astype(jnp.bfloat16)
        counts = mm(oh_hi, oh_lo, NT)
        counts_t = mm(oh_lo, oh_hi, NT)
        for h in range(16):
            at = slice(h * 128, (h + 1) * 128)
            scaled = t_ref[:, at].astype(jnp.float32) * counts[h:h + 1, :]
            ct_ref[:, at] = split2(scaled)

        source = mm(s_ref[...], ohs_ref[...])
        target = mm(t_ref[...], ohd_ref[...])
        x = rows_ref[:, 0, :].T[:HPAD]
        y = rows_ref[:, 1, :].T[:HPAD]
        a, c = source[:HPAD], source[HPAD:]
        query_b = jnp.concatenate(
            [a * x - c * y, a * y + c * x, jnp.zeros((256 - FEAT, SPAN), jnp.float32)], axis=0
        ).astype(jnp.bfloat16)
        query = query_b[:FEAT].astype(jnp.float32)
        positive = jnp.sum(query * target, axis=0, keepdims=True)
        peak = positive
        for h in range(8):
            at = slice(h * CHUNK, (h + 1) * CHUNK)
            count = jnp.concatenate([counts_t[:, 2 * h:2 * h + 1], counts_t[:, 2 * h + 1:2 * h + 2]], axis=0)
            scores = mm(tn_ref[at, :], query_b)
            scores = jnp.where(count > 0.0, scores, -1e30)
            sc_ref[at, :] = scores
            peak = jnp.maximum(peak, jnp.max(scores, axis=0, keepdims=True))
        pos_exp = jnp.exp(positive - peak)
        total = pos_exp
        for h in range(8):
            at = slice(h * CHUNK, (h + 1) * CHUNK)
            count = jnp.concatenate([counts_t[:, 2 * h:2 * h + 1], counts_t[:, 2 * h + 1:2 * h + 2]], axis=0)
            e = jnp.exp(sc_ref[at, :] - peak)
            sc_ref[at, :] = e
            total = total + jnp.sum(e * count, axis=0, keepdims=True)
        inv = 1.0 / total
        live = jnp.where(
            lax.broadcasted_iota(jnp.int32, (1, SPAN), 1) + b * SPAN < live_here, 1.0, 0.0
        )
        coef = (pos_exp * inv - 1.0) * live
        inv = inv * live
        for h in range(8):
            at = slice(h * CHUNK, (h + 1) * CHUNK)
            w_ref[at, :] = (sc_ref[at, :] * inv).astype(jnp.bfloat16)
        both = mm(ct_ref[...], w_ref[...])
        grad_q = both[:FEAT] + both[FEAT:] + coef * target
        pos_q = split2(coef * query)
        g, k = grad_q[:HPAD], grad_q[HPAD:]
        grad_s = split2(jnp.concatenate([g * x + k * y, k * x - g * y], axis=0))
        relrow = relf_ref[b]
        first = lax.broadcasted_iota(jnp.int32, (24, SPAN), 0) == 0
        perm_ref[:, 0, :] = jnp.concatenate(
            [g * a + k * c, jnp.where(first, relrow, 0.0)], axis=0
        ).T
        perm_ref[:, 1, :] = jnp.concatenate(
            [k * a - g * c, jnp.zeros((24, SPAN), jnp.float32)], axis=0
        ).T

        def place_row(j, cc):
            sort_ref[pos_ref[b * SPAN + j]] = perm_ref[j]
            return cc

        lax.fori_loop(0, SPAN, place_row, 0, unroll=16)
        for h in range(8):
            at = slice(h * CHUNK, (h + 1) * CHUNK)
            oh = ohs_ref[at, :]
            back = mm(grad_s, oh, NT)
            ent_ref[:FEAT, at] += back[:FEAT] + back[FEAT:]
            neg = mm(query_b[:FEAT], w_ref[at, :], NT)
            pos = mm(pos_q, ohd_ref[at, :], NT)
            count = jnp.concatenate([counts[2 * h:2 * h + 1, :], counts[2 * h + 1:2 * h + 2, :]], axis=1)
            ent_ref[FEAT:, at] += neg * count + (pos[:FEAT] + pos[FEAT:])
        return carry

    lax.fori_loop(0, live_blocks, block, 0)

    def tile(t, carry):
        begin = tile_ref[t]
        size = tile_ref[RTILES + t]

        def piece(n, acc):
            base = begin + n * RTILE
            left = size - n * RTILE
            ok = lax.broadcasted_iota(jnp.int32, (RTILE, 128), 0) < left
            re = jnp.where(ok, sort_ref[pl.ds(base, RTILE), 0, :], 0.0).T
            im = jnp.where(ok, sort_ref[pl.ds(base, RTILE), 1, :], 0.0).T
            names = re[HPAD:HPAD + 1, :].astype(jnp.int32)
            oh = jnp.where(
                lax.broadcasted_iota(jnp.int32, (RTILE, RTILE), 0) + t * RTILE == names, 1.0, 0.0
            ).astype(jnp.bfloat16)
            part = mm(split2(jnp.concatenate([re[:HPAD], im[:HPAD]], axis=0)), oh, NT)
            return acc + part[:FEAT] + part[FEAT:]

        acc = lax.fori_loop(
            0, (size + RTILE - 1) // RTILE, piece, jnp.zeros((FEAT, RTILE), jnp.float32)
        )
        rel_ref[:, pl.ds(pl.multiple_of(t * RTILE, RTILE), RTILE)] = acc
        return carry

    lax.fori_loop(0, RTILES, tile, 0)


def edge_call(meta, relid, pos, tiles, src, dst, neg, relf, s_t, t_t, table):
    smem = pl.BlockSpec(memory_space=pltpu.SMEM)
    vmem = pl.BlockSpec(memory_space=pltpu.VMEM)
    return pl.pallas_call(
        edge_kernel,
        out_shape=(
            jax.ShapeDtypeStruct((2 * FEAT, ROWS), jnp.float32),
            jax.ShapeDtypeStruct((FEAT, RTILES * RTILE), jnp.float32),
        ),
        in_specs=[smem] * 4 + [vmem] * 7,
        out_specs=(vmem, vmem),
        scratch_shapes=[
            pltpu.VMEM((ROWS, 256), jnp.bfloat16),
            pltpu.VMEM((ROWS, SPAN), jnp.float32),
            pltpu.VMEM((ROWS, SPAN), jnp.bfloat16),
            pltpu.VMEM((ROWS, SPAN), jnp.bfloat16),
            pltpu.VMEM((ROWS, SPAN), jnp.bfloat16),
            pltpu.VMEM((2 * FEAT, ROWS), jnp.bfloat16),
            pltpu.VMEM((SPAN, 2, 128), jnp.float32),
            pltpu.VMEM((SPAN, 2, 128), jnp.float32),
            pltpu.VMEM((SLOTS + RTILE, 2, 128), jnp.float32),
        ],
        compiler_params=pltpu.CompilerParams(vmem_limit_bytes=56 * 1024 * 1024),
        name="edges",
    )(meta, relid, pos, tiles, src, dst, neg, relf, s_t, t_t, table)


def place(ids):
    return ((ids >> 3) & 7) * 256 + (ids >> 6) * 8 + (ids & 7)


def bucket(relid, live_blocks):
    which = relid >> 8
    valid = (jnp.arange(SLOTS, dtype=jnp.int32) < live_blocks * SPAN)[:, None]
    one = ((which[:, None] == jnp.arange(RTILES, dtype=jnp.int32)[None]) & valid).astype(jnp.bfloat16)
    grid = one.reshape(SLOTS // 128, 128, RTILES)
    tri = (jnp.arange(128)[:, None] > jnp.arange(128)[None]).astype(jnp.bfloat16)
    inner = jnp.einsum("ij,cjt->cit", tri, grid, preferred_element_type=jnp.float32)
    sums = jnp.sum(grid.astype(jnp.float32), axis=1)
    outer = jnp.cumsum(sums, axis=0) - sums
    size = jnp.sum(sums, axis=0)
    begin = jnp.cumsum(size) - size
    where = inner + (outer + begin[None])[:, None, :]
    pos = jnp.sum(where * grid.astype(jnp.float32), axis=2).reshape(SLOTS).astype(jnp.int32)
    return pos, jnp.concatenate([begin, size]).astype(jnp.int32)


def halves(v):
    pad = [(0, 0)] * (v.ndim - 1) + [(0, HPAD - HALF)]
    return jnp.concatenate([jnp.pad(v[..., :HALF], pad), jnp.pad(v[..., HALF:], pad)], axis=-1)


def rel_table(relations):
    return jnp.pad(relations.reshape(NREL, 2, HALF), ((0, 0), (0, 0), (0, 128 - HALF)))


def edge_work(s_t, t_t, relations, edge_src, edge_rel, edge_dst, negatives, live_count, first_slot):
    live_here = live_count - first_slot
    live_blocks = jnp.clip((live_here + SPAN - 1) // SPAN, 0, SPANS_DEV)
    meta = jnp.stack([live_blocks, live_here])
    pos, tiles = bucket(edge_rel, live_blocks)
    return edge_call(
        meta, edge_rel, pos, tiles,
        place(edge_src).reshape(SPANS_DEV, 1, SPAN),
        place(edge_dst).reshape(SPANS_DEV, 1, SPAN),
        place(negatives).reshape(SPANS_DEV, 1, 1024),
        edge_rel.astype(jnp.float32).reshape(SPANS_DEV, 1, SPAN),
        s_t, t_t, rel_table(relations),
    )


def unhalve(v):
    return jnp.concatenate([v[..., :HALF], v[..., HPAD:HPAD + HALF]], axis=-1)


def local(entities, relations, edge_src, edge_rel, edge_dst, negatives, pair_live, pair_plan):
    pair_count = lax.axis_size("pair")
    edge_index = lax.axis_index("edge")
    outgoing = halves(entities[jnp.transpose(pair_plan)])
    arrived = lax.all_to_all(outgoing, "pair", split_axis=1, concat_axis=1, tiled=True)
    owned = jnp.transpose(arrived.reshape(2, CHUNK, FEAT), (0, 2, 1))
    blocks = lax.all_gather(owned, "edge", axis=2, tiled=True)
    ent, rel = edge_work(
        blocks[0], blocks[1], relations, edge_src[0], edge_rel[0], edge_dst[0], negatives[0],
        pair_live[0], edge_index * SLOTS,
    )
    summed = lax.psum_scatter(ent, "edge", scatter_dimension=1, tiled=True)
    rows = jnp.transpose(summed.reshape(2, FEAT, CHUNK), (0, 2, 1)).reshape(2, pair_count, 8, FEAT)
    returned = lax.all_to_all(rows, "pair", split_axis=1, concat_axis=1, tiled=True)
    where = jnp.argsort(jnp.transpose(pair_plan).reshape(-1))
    ent_grad = unhalve(returned.reshape(2 * pair_count, 8, FEAT)[where])
    rel_grad = lax.psum(unhalve(rel.T)[:NREL], ("pair", "edge"))
    return ent_grad, rel_grad


def solution(mesh):
    placed = (
        P(None, ("pair", "edge"), None),
        P(),
        P("pair", "edge"),
        P("pair", "edge"),
        P("pair", "edge"),
        P("pair", "edge", None),
        P("pair"),
        P(),
    )
    return jax.shard_map(
        local,
        mesh=mesh,
        in_specs=placed,
        out_specs=(P(None, ("pair", "edge"), None), P()),
        check_vma=False,
    )
```

```python
import functools
import jax
import jax.numpy as jnp
from jax import lax
from jax.experimental import pallas as pl
from jax.experimental.pallas import tpu as pltpu
from jax.sharding import PartitionSpec as P

DIM = 200
HALF = 100
HPAD = 104
FEAT = 208
NREL = 4131
RTILE = 256
RTILES = 17
SPAN = 512
SPANS_DEV = 8
SLOTS = SPAN * SPANS_DEV
ROWS = 2048
CHUNK = 256
NN = (((1,), (0,)), ((), ()))
NT = (((1,), (1,)), ((), ()))
MESH = pl.DeviceIdType.MESH


def mm(a, b, dims=NN):
    return lax.dot_general(a, b, dims, preferred_element_type=jnp.float32)


def split2(v):
    hi = v.astype(jnp.bfloat16)
    lo = (v - hi.astype(jnp.float32)).astype(jnp.bfloat16)
    return jnp.concatenate([hi, lo], axis=0)


def edge_kernel(
    meta_ref, relid_ref, pos_ref, tile_ref,
    src_ref, dst_ref, neg_ref, relf_ref, s_ref, t_ref, table_ref,
    ent_ref, rel_ref,
    tn_ref, sc_ref, w_ref, ohs_ref, ohd_ref, ct_ref, rows_ref, perm_ref, sort_ref,
):
    live_blocks = meta_ref[0]
    live_here = meta_ref[1]
    ent_ref[...] = jnp.zeros_like(ent_ref)
    for h in range(ROWS // CHUNK):
        part = t_ref[:, h * CHUNK:(h + 1) * CHUNK].astype(jnp.float32)
        part = jnp.concatenate([part, jnp.zeros((256 - FEAT, CHUNK), jnp.float32)], axis=0)
        tn_ref[h * CHUNK:(h + 1) * CHUNK, :] = part.T.astype(jnp.bfloat16)

    def block(b, carry):
        def fetch_row(j, c):
            rows_ref[j] = table_ref[relid_ref[b * SPAN + j]]
            return c

        lax.fori_loop(0, SPAN, fetch_row, 0, unroll=16)
        src_row = src_ref[b]
        dst_row = dst_ref[b]
        neg_row = neg_ref[b]
        for h in range(ROWS // CHUNK):
            ids = lax.broadcasted_iota(jnp.int32, (CHUNK, SPAN), 0) + h * CHUNK
            at = pl.ds(h * CHUNK, CHUNK)
            ohs_ref[at, :] = jnp.where(ids == src_row, 1.0, 0.0).astype(jnp.bfloat16)
            ohd_ref[at, :] = jnp.where(ids == dst_row, 1.0, 0.0).astype(jnp.bfloat16)
        neg_hi = neg_row // 128
        neg_lo = neg_row - neg_hi * 128
        oh_hi = jnp.where(lax.broadcasted_iota(jnp.int32, (16, 1024), 0) == neg_hi, 1.0, 0.0).astype(jnp.bfloat16)
        oh_lo = jnp.where(lax.broadcasted_iota(jnp.int32, (128, 1024), 0) == neg_lo, 1.0, 0.0).astype(jnp.bfloat16)
        counts = mm(oh_hi, oh_lo, NT)
        counts_t = mm(oh_lo, oh_hi, NT)
        for h in range(16):
            at = slice(h * 128, (h + 1) * 128)
            scaled = t_ref[:, at].astype(jnp.float32) * counts[h:h + 1, :]
            ct_ref[:, at] = split2(scaled)

        source = mm(s_ref[...], ohs_ref[...])
        target = mm(t_ref[...], ohd_ref[...])
        x = rows_ref[:, 0, :].T[:HPAD]
        y = rows_ref[:, 1, :].T[:HPAD]
        a, c = source[:HPAD], source[HPAD:]
        query_b = jnp.concatenate(
            [a * x - c * y, a * y + c * x, jnp.zeros((256 - FEAT, SPAN), jnp.float32)], axis=0
        ).astype(jnp.bfloat16)
        query = query_b[:FEAT].astype(jnp.float32)
        positive = jnp.sum(query * target, axis=0, keepdims=True)
        peak = positive
        for h in range(8):
            at = slice(h * CHUNK, (h + 1) * CHUNK)
            count = jnp.concatenate([counts_t[:, 2 * h:2 * h + 1], counts_t[:, 2 * h + 1:2 * h + 2]], axis=0)
            scores = mm(tn_ref[at, :], query_b)
            scores = jnp.where(count > 0.0, scores, -1e30)
            sc_ref[at, :] = scores
            peak = jnp.maximum(peak, jnp.max(scores, axis=0, keepdims=True))
        pos_exp = jnp.exp(positive - peak)
        total = pos_exp
        for h in range(8):
            at = slice(h * CHUNK, (h + 1) * CHUNK)
            count = jnp.concatenate([counts_t[:, 2 * h:2 * h + 1], counts_t[:, 2 * h + 1:2 * h + 2]], axis=0)
            e = jnp.exp(sc_ref[at, :] - peak)
            sc_ref[at, :] = e
            total = total + jnp.sum(e * count, axis=0, keepdims=True)
        inv = 1.0 / total
        live = jnp.where(
            lax.broadcasted_iota(jnp.int32, (1, SPAN), 1) + b * SPAN < live_here, 1.0, 0.0
        )
        coef = (pos_exp * inv - 1.0) * live
        inv = inv * live
        for h in range(8):
            at = slice(h * CHUNK, (h + 1) * CHUNK)
            w_ref[at, :] = (sc_ref[at, :] * inv).astype(jnp.bfloat16)
        both = mm(ct_ref[...], w_ref[...])
        grad_q = both[:FEAT] + both[FEAT:] + coef * target
        pos_q = split2(coef * query)
        g, k = grad_q[:HPAD], grad_q[HPAD:]
        grad_s = split2(jnp.concatenate([g * x + k * y, k * x - g * y], axis=0))
        relrow = relf_ref[b]
        first = lax.broadcasted_iota(jnp.int32, (24, SPAN), 0) == 0
        perm_ref[:, 0, :] = jnp.concatenate(
            [g * a + k * c, jnp.where(first, relrow, 0.0)], axis=0
        ).T
        perm_ref[:, 1, :] = jnp.concatenate(
            [k * a - g * c, jnp.zeros((24, SPAN), jnp.float32)], axis=0
        ).T

        def place_row(j, cc):
            sort_ref[pos_ref[b * SPAN + j]] = perm_ref[j]
            return cc

        lax.fori_loop(0, SPAN, place_row, 0, unroll=16)
        for h in range(8):
            at = slice(h * CHUNK, (h + 1) * CHUNK)
            oh = ohs_ref[at, :]
            back = mm(grad_s, oh, NT)
            ent_ref[h, :FEAT, :] += back[:FEAT] + back[FEAT:]
            neg = mm(query_b[:FEAT], w_ref[at, :], NT)
            pos = mm(pos_q, ohd_ref[at, :], NT)
            count = jnp.concatenate([counts[2 * h:2 * h + 1, :], counts[2 * h + 1:2 * h + 2, :]], axis=1)
            ent_ref[h, FEAT:, :] += neg * count + (pos[:FEAT] + pos[FEAT:])
        return carry

    lax.fori_loop(0, live_blocks, block, 0)

    def tile(t, carry):
        begin = tile_ref[t]
        size = tile_ref[RTILES + t]

        def piece(n, acc):
            base = begin + n * RTILE
            left = size - n * RTILE
            ok = lax.broadcasted_iota(jnp.int32, (RTILE, 128), 0) < left
            re = jnp.where(ok, sort_ref[pl.ds(base, RTILE), 0, :], 0.0).T
            im = jnp.where(ok, sort_ref[pl.ds(base, RTILE), 1, :], 0.0).T
            names = re[HPAD:HPAD + 1, :].astype(jnp.int32)
            oh = jnp.where(
                lax.broadcasted_iota(jnp.int32, (RTILE, RTILE), 0) + t * RTILE == names, 1.0, 0.0
            ).astype(jnp.bfloat16)
            part = mm(split2(jnp.concatenate([re[:HPAD], im[:HPAD]], axis=0)), oh, NT)
            return acc + part[:FEAT] + part[FEAT:]

        acc = lax.fori_loop(
            0, (size + RTILE - 1) // RTILE, piece, jnp.zeros((FEAT, RTILE), jnp.float32)
        )
        rel_ref[pl.ds(52 * t, 26)] = acc[:, :128].reshape(26, 8, 128)
        rel_ref[pl.ds(52 * t + 26, 26)] = acc[:, 128:].reshape(26, 8, 128)
        return carry

    lax.fori_loop(0, RTILES, tile, 0)
    rel_ref[884:] = jnp.zeros((12, 8, 128), jnp.float32)


def edge_call(meta, relid, pos, tiles, src, dst, neg, relf, s_t, t_t, table):
    smem = pl.BlockSpec(memory_space=pltpu.SMEM)
    vmem = pl.BlockSpec(memory_space=pltpu.VMEM)
    return pl.pallas_call(
        edge_kernel,
        out_shape=(
            jax.ShapeDtypeStruct((8, 2 * FEAT, CHUNK), jnp.float32),
            jax.ShapeDtypeStruct((896, 8, 128), jnp.float32),
        ),
        in_specs=[smem] * 4 + [vmem] * 7,
        out_specs=(vmem, vmem),
        scratch_shapes=[
            pltpu.VMEM((ROWS, 256), jnp.bfloat16),
            pltpu.VMEM((ROWS, SPAN), jnp.float32),
            pltpu.VMEM((ROWS, SPAN), jnp.bfloat16),
            pltpu.VMEM((ROWS, SPAN), jnp.bfloat16),
            pltpu.VMEM((ROWS, SPAN), jnp.bfloat16),
            pltpu.VMEM((2 * FEAT, ROWS), jnp.bfloat16),
            pltpu.VMEM((SPAN, 2, 128), jnp.float32),
            pltpu.VMEM((SPAN, 2, 128), jnp.float32),
            pltpu.VMEM((SLOTS + RTILE, 2, 128), jnp.float32),
        ],
        compiler_params=pltpu.CompilerParams(vmem_limit_bytes=56 * 1024 * 1024),
        name="edges",
    )(meta, relid, pos, tiles, src, dst, neg, relf, s_t, t_t, table)


def place(ids):
    return ((ids >> 3) & 7) * 256 + (ids >> 6) * 8 + (ids & 7)


def bucket(relid, live_blocks):
    which = relid >> 8
    valid = (jnp.arange(SLOTS, dtype=jnp.int32) < live_blocks * SPAN)[:, None]
    one = ((which[:, None] == jnp.arange(RTILES, dtype=jnp.int32)[None]) & valid).astype(jnp.bfloat16)
    grid = one.reshape(SLOTS // 128, 128, RTILES)
    tri = (jnp.arange(128)[:, None] > jnp.arange(128)[None]).astype(jnp.bfloat16)
    inner = jnp.einsum("ij,cjt->cit", tri, grid, preferred_element_type=jnp.float32)
    sums = jnp.sum(grid.astype(jnp.float32), axis=1)
    outer = jnp.cumsum(sums, axis=0) - sums
    size = jnp.sum(sums, axis=0)
    begin = jnp.cumsum(size) - size
    where = inner + (outer + begin[None])[:, None, :]
    pos = jnp.sum(where * grid.astype(jnp.float32), axis=2).reshape(SLOTS).astype(jnp.int32)
    return pos, jnp.concatenate([begin, size]).astype(jnp.int32)


def halves(v):
    pad = [(0, 0)] * (v.ndim - 1) + [(0, HPAD - HALF)]
    return jnp.concatenate([jnp.pad(v[..., :HALF], pad), jnp.pad(v[..., HALF:], pad)], axis=-1)


def rel_table(relations):
    return jnp.pad(relations.reshape(NREL, 2, HALF), ((0, 0), (0, 0), (0, 128 - HALF)))


def edge_work(s_t, t_t, relations, edge_src, edge_rel, edge_dst, negatives, live_count, first_slot):
    live_here = live_count - first_slot
    live_blocks = jnp.clip((live_here + SPAN - 1) // SPAN, 0, SPANS_DEV)
    meta = jnp.stack([live_blocks, live_here])
    pos, tiles = bucket(edge_rel, live_blocks)
    return edge_call(
        meta, edge_rel, pos, tiles,
        place(edge_src).reshape(SPANS_DEV, 1, SPAN),
        place(edge_dst).reshape(SPANS_DEV, 1, SPAN),
        place(negatives).reshape(SPANS_DEV, 1, 1024),
        edge_rel.astype(jnp.float32).reshape(SPANS_DEV, 1, SPAN),
        s_t, t_t, rel_table(relations),
    )


RINGS = 104
TILE7 = 7


def exchange_kernel(
    g_ref, r_ref, ent_ref, rel_ref,
    ring_ref, core_ref, acc_ref, hyp_ref, zb_ref, zr_ref, zf_ref, out_ref,
    ring_s, ring_r, core_s, core_r, hyp_s, hyp_r, zs_s, zs_r, za_s, za_r,
    ag_s, ag_r, last_s, last_r, a2a_s, a2a_r,
):
    p = lax.axis_index("pair")
    e = lax.axis_index("edge")
    core = p % 2
    chip = p // 2
    x = chip // 4
    y = chip % 4

    def at(xx, yy):
        return ((xx * 4 + yy) * 2 + core, e)

    partner = {
        "x1": at(x + 1 - 2 * (x % 2), y),
        "x2": at(3 - x, y),
        "y1": at(x, y + 1 - 2 * (y % 2)),
        "y2": at(x, 3 - y),
    }
    bit = {
        "x1": (x // 2 + x % 2) % 2,
        "x2": x // 2,
        "y1": (y // 2 + y % 2) % 2,
        "y2": y // 2,
    }
    order = [
        ("x1", "y1", "x2", "y2"),
        ("y1", "x2", "y2", "x1"),
        ("x2", "y2", "x1", "y1"),
        ("y2", "x1", "y1", "x2"),
    ]
    sibling = (p + 1 - 2 * core, e)

    barrier = pltpu.get_barrier_semaphore()
    for d in range(1, 32):
        pl.semaphore_signal(barrier, inc=1, device_id=((p + d) % 32, e), device_id_type=MESH)
    for d in range(1, 8):
        pl.semaphore_signal(barrier, inc=1, device_id=(p, (e + d) % 8), device_id_type=MESH)
    pl.semaphore_wait(barrier, 38)

    sent = []

    def push(src, dst, ss, rs, device):
        copy = pltpu.make_async_remote_copy(
            src_ref=src, dst_ref=dst, send_sem=ss, recv_sem=rs, device_id=device, device_id_type=MESH
        )
        copy.start()
        sent.append(copy)
        return copy

    streams = [(0, 0), (208, 1), (104, 0), (312, 1)]
    ring = {}

    def chunk(down, s):
        return (e + 1 + s) % 8 if down else (e + 7 - s) % 8

    def ring_send(s):
        for i, (row, down) in enumerate(streams):
            c = chunk(down, s)
            if s == 0:
                src = g_ref.at[c, pl.ds(row, RINGS)]
            else:
                ring[i].wait_recv()
                ring_ref[i, s - 1] += g_ref[c, pl.ds(row, RINGS), :]
                src = ring_ref.at[i, s - 1]
            to = (p, (e + 7) % 8) if down else (p, (e + 1) % 8)
            ring[i] = push(src, ring_ref.at[i, s], ring_s.at[i, s], ring_r.at[i, s], to)

    moves = {}
    off = [0, 0, 0, 0]
    offs = [[], [], [], []]
    base = [0, 8, 12, 14]

    def hyp_send(k, s):
        half = 8 >> s
        b = bit[order[k][s]]
        moves[k] = push(
            acc_ref.at[k, pl.ds(off[k] + (1 - b) * half, half)],
            hyp_ref.at[k, pl.ds(base[s], half)],
            hyp_s.at[k, s], hyp_r.at[k, s], partner[order[k][s]],
        )
        off[k] = off[k] + b * half
        offs[k].append(off[k])

    def hyp_take(k, s):
        half = 8 >> s
        moves[k].wait_recv()
        acc_ref[k, pl.ds(off[k], half)] += hyp_ref[k, pl.ds(base[s], half)]

    cores = [
        push(r_ref.at[1 - core, k], core_ref.at[k], core_s.at[k], core_r.at[k], sibling)
        for k in range(4)
    ]
    ring_send(0)
    for k in range(4):
        cores[k].wait_recv()
        acc_ref[k] = r_ref[core, k] + core_ref[k]
        hyp_send(k, 0)
    ring_send(1)

    def hyp_step(s):
        for k in range(4):
            hyp_take(k, s)
            if s < 3:
                hyp_send(k, s + 1)

    hyp_step(0)
    ring_send(2)
    hyp_step(1)
    hyp_step(2)
    ring_send(3)
    hyp_step(3)
    for t in range(TILE7):
        for k in range(4):
            zb_ref[t, k] = acc_ref[k, off[k], t]
    zb_ref[TILE7] = jnp.zeros((4, 8, 128), jnp.float32)
    zs = [
        push(zb_ref.at[(e + d) % 8], zr_ref.at[d], zs_s.at[d], zs_r.at[d], (p, (e + d) % 8))
        for d in range(1, 8)
    ]
    ring_send(4)
    total = zb_ref[e]
    for d in range(1, 8):
        zs[d - 1].wait_recv()
        total = total + zr_ref[d]
    zf_ref[e] = total
    za = [
        push(zf_ref.at[e], zf_ref.at[e], za_s.at[d], za_r.at[d], (p, (e + d) % 8))
        for d in range(1, 8)
    ]
    ring_send(5)
    for c in za:
        c.wait_recv()
    for t in range(TILE7):
        for k in range(4):
            rel_ref[core, k, off[k], t] = zf_ref[t, k]

    def gather_send(k, s):
        half = 8 >> s
        span = rel_ref.at[core, k, pl.ds(offs[k][s], half)]
        moves[k] = push(span, span, ag_s.at[k, s], ag_r.at[k, s], partner[order[k][s]])

    def gather_step(s):
        for k in range(4):
            moves[k].wait_recv()
            if s > 0:
                gather_send(k, s - 1)
            else:
                span = rel_ref.at[core, k]
                moves[k] = push(span, span, last_s.at[k], last_r.at[k], sibling)

    for k in range(4):
        gather_send(k, 3)
    gather_step(3)
    ring_send(6)
    gather_step(2)

    for half in range(2):
        parts = []
        for i, (row, down) in enumerate(streams):
            if down == half:
                ring[i].wait_recv()
                parts.append(ring_ref[i, 6] + g_ref[e, pl.ds(row, RINGS), :])
        full = jnp.concatenate(
            [parts[0][:HALF], parts[1][:HALF], jnp.zeros((56, CHUNK), jnp.float32)], axis=0
        ).T
        for n in range(32):
            out_ref[n, half] = full[n * 8:(n + 1) * 8, :]
    swap = [
        push(out_ref.at[(p + d) % 32], ent_ref.at[p], a2a_s.at[d], a2a_r.at[d], ((p + d) % 32, e))
        for d in range(1, 32)
    ]
    ent_ref[p] = out_ref[p]
    gather_step(1)
    gather_step(0)
    for c in swap:
        c.wait_recv()
    for k in range(4):
        moves[k].wait_recv()
    for c in sent:
        c.wait_send()


def exchange(g, r):
    vmem = pl.BlockSpec(memory_space=pltpu.VMEM)
    f32 = jnp.float32
    dma = pltpu.SemaphoreType.DMA
    return pl.pallas_call(
        exchange_kernel,
        out_shape=(
            jax.ShapeDtypeStruct((32, 2, 8, CHUNK), f32),
            jax.ShapeDtypeStruct((2, 4, 16, TILE7, 8, 128), f32),
        ),
        in_specs=[vmem] * 2,
        out_specs=(vmem, vmem),
        scratch_shapes=[
            pltpu.VMEM((4, 7, RINGS, CHUNK), f32),
            pltpu.VMEM((4, 16, TILE7, 8, 128), f32),
            pltpu.VMEM((4, 16, TILE7, 8, 128), f32),
            pltpu.VMEM((4, 15, TILE7, 8, 128), f32),
            pltpu.VMEM((8, 4, 8, 128), f32),
            pltpu.VMEM((8, 4, 8, 128), f32),
            pltpu.VMEM((8, 4, 8, 128), f32),
            pltpu.VMEM((32, 2, 8, CHUNK), f32),
            dma((4, 7)), dma((4, 7)), dma((4,)), dma((4,)), dma((4, 4)), dma((4, 4)),
            dma((8,)), dma((8,)), dma((8,)), dma((8,)),
            dma((4, 4)), dma((4, 4)), dma((4,)), dma((4,)), dma((32,)), dma((32,)),
        ],
        compiler_params=pltpu.CompilerParams(
            collective_id=0, has_side_effects=True, vmem_limit_bytes=48 * 1024 * 1024
        ),
        name="exchange",
    )(g, r)


def finish_kernel(plan_ref, ent_ref, rel_ref, out_ref, rel_out_ref):
    def put(i, c):
        out_ref[plan_ref[i]] = ent_ref[i][:, :DIM]
        return c

    lax.fori_loop(0, 64, put, 0, unroll=8)

    def turn(n):
        v = rel_ref[pl.ds(n * 26, 26)].reshape(FEAT, 128)
        v = jnp.concatenate([v[:HALF], v[HPAD:HPAD + HALF], jnp.zeros((56, 128), jnp.float32)], axis=0)
        return v.T[:, :DIM]

    def rows(n, c):
        rel_out_ref[pl.ds(pl.multiple_of(n * 128, 128), 128), :] = turn(n)
        return c

    lax.fori_loop(0, 32, rows, 0, unroll=4)
    rel_out_ref[4096:NREL, :] = turn(32)[: NREL - 4096]


def finish(plan, ent, rel):
    vmem = pl.BlockSpec(memory_space=pltpu.VMEM)
    return pl.pallas_call(
        finish_kernel,
        out_shape=(
            jax.ShapeDtypeStruct((64, 8, DIM), jnp.float32),
            jax.ShapeDtypeStruct((NREL, DIM), jnp.float32),
        ),
        in_specs=[pl.BlockSpec(memory_space=pltpu.SMEM), vmem, vmem],
        out_specs=(vmem, vmem),
        compiler_params=pltpu.CompilerParams(vmem_limit_bytes=32 * 1024 * 1024),
        name="finish",
    )(plan, ent, rel)


def local(entities, relations, edge_src, edge_rel, edge_dst, negatives, pair_live, pair_plan):
    edge_index = lax.axis_index("edge")
    outgoing = halves(entities[jnp.transpose(pair_plan)])
    arrived = lax.all_to_all(outgoing, "pair", split_axis=1, concat_axis=1, tiled=True)
    owned = jnp.transpose(arrived.reshape(2, CHUNK, FEAT), (0, 2, 1))
    blocks = lax.all_gather(owned, "edge", axis=2, tiled=True)
    ent, rel = edge_work(
        blocks[0], blocks[1], relations, edge_src[0], edge_rel[0], edge_dst[0], negatives[0],
        pair_live[0], edge_index * SLOTS,
    )
    returned, rel_tiles = exchange(ent, rel.reshape(2, 4, 16, TILE7, 8, 128))
    return finish(pair_plan.reshape(-1), returned.reshape(64, 8, CHUNK), rel_tiles.reshape(896, 8, 128))


def solution(mesh):
    placed = (
        P(None, ("pair", "edge"), None),
        P(),
        P("pair", "edge"),
        P("pair", "edge"),
        P("pair", "edge"),
        P("pair", "edge", None),
        P("pair"),
        P(),
    )
    return jax.shard_map(
        local,
        mesh=mesh,
        in_specs=placed,
        out_specs=(P(None, ("pair", "edge"), None), P()),
        check_vma=False,
    )
```

```python
import functools
import jax
import jax.numpy as jnp
from jax import lax
from jax.experimental import pallas as pl
from jax.experimental.pallas import tpu as pltpu
from jax.sharding import PartitionSpec as P

DIM = 200
HALF = 100
HPAD = 104
FEAT = 208
NREL = 4131
RTILE = 256
RTILES = 17
SPAN = 512
SPANS_DEV = 8
SLOTS = SPAN * SPANS_DEV
ROWS = 2048
CHUNK = 256
NN = (((1,), (0,)), ((), ()))
NT = (((1,), (1,)), ((), ()))
MESH = pl.DeviceIdType.MESH


def mm(a, b, dims=NN):
    return lax.dot_general(a, b, dims, preferred_element_type=jnp.float32)


def split2(v):
    hi = v.astype(jnp.bfloat16)
    lo = (v - hi.astype(jnp.float32)).astype(jnp.bfloat16)
    return jnp.concatenate([hi, lo], axis=0)


def place(ids):
    owner = ids // 64
    left = ids - owner * 64
    edge = left // 8
    return edge * 256 + owner * 8 + (left - edge * 8)


def edge_kernel(
    live_ref, pos_ref, tile_ref,
    src_ref, dst_ref, neg_ref, relid_ref, tab_ref, tn_ref, xy_ref,
    ent_ref, rel_ref,
    sc_ref, w_ref, ohs_ref, ohd_ref, ct_ref, perm_ref, sort_ref,
):
    live_here = live_ref[0] - lax.axis_index("edge") * SLOTS
    ent_ref[...] = jnp.zeros_like(ent_ref)
    s_ref = tab_ref.at[0]
    t_ref = tab_ref.at[1]

    def block(b, carry):
        at = pl.ds(pl.multiple_of(b * SPAN, SPAN), SPAN)
        src_row = place(src_ref[:, at])
        dst_row = place(dst_ref[:, at])
        neg_row = place(neg_ref[0, pl.ds(b, 1), :])
        for h in range(ROWS // CHUNK):
            ids = lax.broadcasted_iota(jnp.int32, (CHUNK, SPAN), 0) + h * CHUNK
            at = pl.ds(h * CHUNK, CHUNK)
            ohs_ref[at, :] = jnp.where(ids == src_row, 1.0, 0.0).astype(jnp.bfloat16)
            ohd_ref[at, :] = jnp.where(ids == dst_row, 1.0, 0.0).astype(jnp.bfloat16)
        neg_hi = neg_row // 128
        neg_lo = neg_row - neg_hi * 128
        oh_hi = jnp.where(lax.broadcasted_iota(jnp.int32, (16, 1024), 0) == neg_hi, 1.0, 0.0).astype(jnp.bfloat16)
        oh_lo = jnp.where(lax.broadcasted_iota(jnp.int32, (128, 1024), 0) == neg_lo, 1.0, 0.0).astype(jnp.bfloat16)
        counts = mm(oh_hi, oh_lo, NT)
        counts_t = mm(oh_lo, oh_hi, NT)
        for h in range(16):
            at = slice(h * 128, (h + 1) * 128)
            scaled = t_ref[:, at].astype(jnp.float32) * counts[h:h + 1, :]
            ct_ref[:, at] = split2(scaled)

        source = mm(s_ref[...], ohs_ref[...])
        target = mm(t_ref[...], ohd_ref[...])
        x = xy_ref[b, :HPAD]
        y = xy_ref[b, HPAD:]
        a, c = source[:HPAD], source[HPAD:]
        query_b = jnp.concatenate(
            [a * x - c * y, a * y + c * x, jnp.zeros((256 - FEAT, SPAN), jnp.float32)], axis=0
        ).astype(jnp.bfloat16)
        query = query_b[:FEAT].astype(jnp.float32)
        positive = jnp.sum(query * target, axis=0, keepdims=True)
        peak = positive
        for h in range(8):
            at = slice(h * CHUNK, (h + 1) * CHUNK)
            count = jnp.concatenate([counts_t[:, 2 * h:2 * h + 1], counts_t[:, 2 * h + 1:2 * h + 2]], axis=0)
            scores = mm(tn_ref[at, :], query_b)
            scores = jnp.where(count > 0.0, scores, -1e30)
            sc_ref[at, :] = scores
            peak = jnp.maximum(peak, jnp.max(scores, axis=0, keepdims=True))
        pos_exp = jnp.exp(positive - peak)
        total = pos_exp
        for h in range(8):
            at = slice(h * CHUNK, (h + 1) * CHUNK)
            count = jnp.concatenate([counts_t[:, 2 * h:2 * h + 1], counts_t[:, 2 * h + 1:2 * h + 2]], axis=0)
            e = jnp.exp(sc_ref[at, :] - peak)
            sc_ref[at, :] = e
            total = total + jnp.sum(e * count, axis=0, keepdims=True)
        inv = 1.0 / total
        live = jnp.where(
            lax.broadcasted_iota(jnp.int32, (1, SPAN), 1) + b * SPAN < live_here, 1.0, 0.0
        )
        coef = (pos_exp * inv - 1.0) * live
        inv = inv * live
        for h in range(8):
            at = slice(h * CHUNK, (h + 1) * CHUNK)
            w_ref[at, :] = (sc_ref[at, :] * inv).astype(jnp.bfloat16)
        both = mm(ct_ref[...], w_ref[...])
        grad_q = both[:FEAT] + both[FEAT:] + coef * target
        pos_q = split2(coef * query)
        g, k = grad_q[:HPAD], grad_q[HPAD:]
        grad_s = split2(jnp.concatenate([g * x + k * y, k * x - g * y], axis=0))
        relrow = relid_ref[:, pl.ds(pl.multiple_of(b * SPAN, SPAN), SPAN)].astype(jnp.float32)
        first = lax.broadcasted_iota(jnp.int32, (24, SPAN), 0) == 0
        perm_ref[:, 0, :] = jnp.concatenate(
            [g * a + k * c, jnp.where(first, relrow, 0.0)], axis=0
        ).T
        perm_ref[:, 1, :] = jnp.concatenate(
            [k * a - g * c, jnp.zeros((24, SPAN), jnp.float32)], axis=0
        ).T

        for n in range(SPAN // 128):
            def place_row(j, cc, n=n):
                sort_ref[pos_ref[b * (SPAN // 128) + n, j]] = perm_ref[n * 128 + j]
                return cc

            lax.fori_loop(0, 128, place_row, 0, unroll=16)
        for h in range(8):
            at = slice(h * CHUNK, (h + 1) * CHUNK)
            oh = ohs_ref[at, :]
            back = mm(grad_s, oh, NT)
            ent_ref[h, :FEAT, :] += back[:FEAT] + back[FEAT:]
            neg = mm(query_b[:FEAT], w_ref[at, :], NT)
            pos = mm(pos_q, ohd_ref[at, :], NT)
            count = jnp.concatenate([counts[2 * h:2 * h + 1, :], counts[2 * h + 1:2 * h + 2, :]], axis=1)
            ent_ref[h, FEAT:, :] += neg * count + (pos[:FEAT] + pos[FEAT:])
        return carry

    lax.fori_loop(0, live_blocks_of(live_here), block, 0)

    def tile(t, carry):
        begin = tile_ref[t, 0]
        size = tile_ref[t, 1]

        def piece(n, acc):
            base = begin + n * RTILE
            left = size - n * RTILE
            ok = lax.broadcasted_iota(jnp.int32, (RTILE, 128), 0) < left
            re = jnp.where(ok, sort_ref[pl.ds(base, RTILE), 0, :], 0.0).T
            im = jnp.where(ok, sort_ref[pl.ds(base, RTILE), 1, :], 0.0).T
            names = re[HPAD:HPAD + 1, :].astype(jnp.int32)
            oh = jnp.where(
                lax.broadcasted_iota(jnp.int32, (RTILE, RTILE), 0) + t * RTILE == names, 1.0, 0.0
            ).astype(jnp.bfloat16)
            part = mm(split2(jnp.concatenate([re[:HPAD], im[:HPAD]], axis=0)), oh, NT)
            return acc + part[:FEAT] + part[FEAT:]

        acc = lax.fori_loop(
            0, (size + RTILE - 1) // RTILE, piece, jnp.zeros((FEAT, RTILE), jnp.float32)
        )
        rel_ref[pl.ds(52 * t, 26)] = acc[:, :128].reshape(26, 8, 128)
        rel_ref[pl.ds(52 * t + 26, 26)] = acc[:, 128:].reshape(26, 8, 128)
        return carry

    lax.fori_loop(0, RTILES, tile, 0)
    rel_ref[884:] = jnp.zeros((12, 8, 128), jnp.float32)


def edge_call(live, pos, tiles, src, dst, neg, relid, tab, tn, xy):
    smem = pl.BlockSpec(memory_space=pltpu.SMEM)
    vmem = pl.BlockSpec(memory_space=pltpu.VMEM)
    return pl.pallas_call(
        edge_kernel,
        out_shape=(
            jax.ShapeDtypeStruct((8, 2 * FEAT, CHUNK), jnp.float32),
            jax.ShapeDtypeStruct((896, 8, 128), jnp.float32),
        ),
        in_specs=[smem] * 3 + [vmem] * 7,
        out_specs=(vmem, vmem),
        scratch_shapes=[
            pltpu.VMEM((ROWS, SPAN), jnp.float32),
            pltpu.VMEM((ROWS, SPAN), jnp.bfloat16),
            pltpu.VMEM((ROWS, SPAN), jnp.bfloat16),
            pltpu.VMEM((ROWS, SPAN), jnp.bfloat16),
            pltpu.VMEM((2 * FEAT, ROWS), jnp.bfloat16),
            pltpu.VMEM((SPAN, 2, 128), jnp.float32),
            pltpu.VMEM((SLOTS + RTILE, 2, 128), jnp.float32),
        ],
        compiler_params=pltpu.CompilerParams(vmem_limit_bytes=56 * 1024 * 1024),
        name="edges",
    )(live, pos, tiles, src, dst, neg, relid, tab, tn, xy)


def fetch_kernel(
    plan_ref, relid_ref, live_ref, relrow_ref, ent_ref, rel_hbm,
    tab_ref, tn_ref, xy_ref, pos_ref, tile_ref,
    relt_ref, table_ref, rows_ref, stage_ref, got_ref, ag_ref,
    rel_sem, a2a_s, a2a_r, ag_s, ag_r,
):
    p = lax.axis_index("pair")
    e = lax.axis_index("edge")
    load = pltpu.make_async_copy(rel_hbm, relt_ref, rel_sem)
    load.start()
    barrier = pltpu.get_barrier_semaphore()
    for d in range(1, 32):
        pl.semaphore_signal(barrier, inc=1, device_id=((p + d) % 32, e), device_id_type=MESH)
    for d in (1, 7):
        pl.semaphore_signal(barrier, inc=1, device_id=(p, (e + d) % 8), device_id_type=MESH)

    gap = jnp.zeros((16, 256 - DIM), jnp.float32)

    def stage(n, c):
        both = jnp.concatenate(
            [ent_ref[plan_ref[0, n]].astype(jnp.float32), ent_ref[plan_ref[1, n]].astype(jnp.float32)], axis=0
        )
        stage_ref[n] = jnp.concatenate([both, gap], axis=1).astype(jnp.bfloat16)
        return c

    lax.fori_loop(0, 32, stage, 0, unroll=4)
    pl.semaphore_wait(barrier, 33)
    sent = []

    def push(src, dst, ss, rs, device):
        copy = pltpu.make_async_remote_copy(
            src_ref=src, dst_ref=dst, send_sem=ss, recv_sem=rs, device_id=device, device_id_type=MESH
        )
        copy.start()
        sent.append(copy)
        return copy

    swap = [
        push(stage_ref.at[(p + d) % 32], got_ref.at[p], a2a_s.at[d], a2a_r.at[d], ((p + d) % 32, e))
        for d in range(1, 32)
    ]
    got_ref[p] = stage_ref[p]

    valid = live_blocks_of(live_ref[0] - e * SLOTS) * SPAN
    ones = []
    total = jnp.zeros((32, 1), jnp.float32)
    sub = lax.broadcasted_iota(jnp.int32, (32, 128), 0)
    lane = lax.broadcasted_iota(jnp.int32, (32, 128), 1)
    for c in range(32):
        which = relrow_ref[:, c * 128:(c + 1) * 128] // RTILE
        one = jnp.where((sub == which) & (lane + c * 128 < valid), 1.0, 0.0)
        size = jnp.sum(one, axis=1, keepdims=True)
        ones.append((one, size))
        total = total + size
    below = jnp.where(
        lax.broadcasted_iota(jnp.int32, (32, 32), 1) < lax.broadcasted_iota(jnp.int32, (32, 32), 0), 1.0, 0.0
    )
    begin = lax.dot_general(
        below, jnp.broadcast_to(total, (32, 128)), NN,
        precision=lax.Precision.HIGHEST, preferred_element_type=jnp.float32,
    )
    tile_ref[...] = jnp.where(lane == 0, begin, total).astype(jnp.int32)
    ahead = jnp.where(
        lax.broadcasted_iota(jnp.int32, (128, 128), 0) < lax.broadcasted_iota(jnp.int32, (128, 128), 1), 1.0, 0.0
    ).astype(jnp.bfloat16)
    for c in range(32):
        one, size = ones[c]
        place = one * (mm(one.astype(jnp.bfloat16), ahead) + begin)
        pos_ref[c:c + 1, :] = jnp.sum(place, axis=0, keepdims=True).astype(jnp.int32)
        begin = begin + size

    load.wait()

    def turn(n, v):
        v = jnp.concatenate([v, jnp.zeros((28, 128), jnp.float32)], axis=0)
        w = jnp.concatenate([v[HALF:DIM], jnp.zeros((28, 128), jnp.float32)], axis=0)
        table_ref[pl.ds(n * 128, 128), 0, :] = v[:128].T
        table_ref[pl.ds(n * 128, 128), 1, :] = w.T

    def build(n, c):
        turn(n, relt_ref[:, pl.ds(pl.multiple_of(n * 128, 128), 128)])
        return c

    lax.fori_loop(0, 32, build, 0, unroll=4)
    tail = jnp.concatenate([relt_ref[:, 4096:NREL], jnp.zeros((DIM, 4224 - NREL), jnp.float32)], axis=1)
    turn(32, tail)

    for c in swap:
        c.wait_recv()
    for s in range(2):
        rows = got_ref[...].astype(jnp.float32)[:, s * 8:(s + 1) * 8, :].reshape(CHUNK, 256)
        cols = rows.T
        zero = jnp.zeros((HPAD - HALF, CHUNK), jnp.float32)
        ag_ref[e, s] = jnp.concatenate([cols[:HALF], zero, cols[HALF:DIM], zero], axis=0).astype(jnp.bfloat16)

    hops = {}

    def forward(h, way, s):
        o = (e + 8 - (h - 1)) % 8 if way == 0 else (e + (h - 1)) % 8
        to = (p, (e + 1) % 8) if way == 0 else (p, (e + 7) % 8)
        hops[way, s] = push(
            ag_ref.at[o, s], ag_ref.at[o, s], ag_s.at[way, s, h - 1], ag_r.at[way, s, h - 1], to
        )

    def settle(o):
        at = pl.ds(pl.multiple_of(o * CHUNK, CHUNK), CHUNK)
        tab_ref[0, :, at] = ag_ref[o, 0]
        tab_ref[1, :, at] = ag_ref[o, 1]
        part = ag_ref[o, 1].astype(jnp.float32)
        part = jnp.concatenate([part, jnp.zeros((256 - FEAT, CHUNK), jnp.float32)], axis=0)
        tn_ref[at, :] = part.T.astype(jnp.bfloat16)

    def relations_of(b):
        def fetch_row(j, c):
            rows_ref[j] = table_ref[relid_ref[0, b * SPAN + j]]
            return c

        lax.fori_loop(0, SPAN, fetch_row, 0, unroll=16)
        xy_ref[b, :HPAD] = jnp.where(keep, rows_ref[:, 0, :].T[:HPAD], 0.0)
        xy_ref[b, HPAD:] = rows_ref[:, 1, :].T[:HPAD]

    keep = lax.broadcasted_iota(jnp.int32, (HPAD, SPAN), 0) < HALF
    all_streams = [(0, 0), (1, 1), (0, 1), (1, 0)]
    for way, s in all_streams:
        forward(1, way, s)
    settle(e)
    relations_of(0)
    relations_of(1)
    for h in range(1, 4):
        for way, s in all_streams:
            hops[way, s].wait_recv()
            if h < 3 or way == s:
                forward(h + 1, way, s)
        settle((e + 8 - h) % 8)
        settle((e + h) % 8)
        relations_of(2 * h)
        relations_of(2 * h + 1)
    hops[0, 0].wait_recv()
    hops[1, 1].wait_recv()
    settle((e + 4) % 8)
    for c in sent:
        c.wait_send()


def live_blocks_of(live_here):
    return jnp.clip((live_here + SPAN - 1) // SPAN, 0, SPANS_DEV)


def fetch(plan, relid, live, entities, relations_t):
    smem = pl.BlockSpec(memory_space=pltpu.SMEM)
    vmem = pl.BlockSpec(memory_space=pltpu.VMEM)
    f32 = jnp.float32
    bf16 = jnp.bfloat16
    dma = pltpu.SemaphoreType.DMA
    return pl.pallas_call(
        fetch_kernel,
        out_shape=(
            jax.ShapeDtypeStruct((2, FEAT, ROWS), bf16),
            jax.ShapeDtypeStruct((ROWS, 256), bf16),
            jax.ShapeDtypeStruct((SPANS_DEV, FEAT, SPAN), f32),
            jax.ShapeDtypeStruct((32, 128), jnp.int32),
            jax.ShapeDtypeStruct((32, 128), jnp.int32),
        ),
        in_specs=[smem, smem, smem, vmem, vmem, pl.BlockSpec(memory_space=pl.ANY)],
        out_specs=(vmem,) * 5,
        scratch_shapes=[
            pltpu.VMEM((DIM, NREL), f32),
            pltpu.VMEM((4224, 2, 128), f32),
            pltpu.VMEM((SPAN, 2, 128), f32),
            pltpu.VMEM((32, 16, 256), bf16),
            pltpu.VMEM((32, 16, 256), bf16),
            pltpu.VMEM((8, 2, FEAT, CHUNK), bf16),
            dma, dma((32,)), dma((32,)), dma((2, 2, 4)), dma((2, 2, 4)),
        ],
        compiler_params=pltpu.CompilerParams(
            collective_id=1, has_side_effects=True, vmem_limit_bytes=48 * 1024 * 1024
        ),
        name="fetch",
    )(plan, relid, live, relid, entities, relations_t)


RINGS = 104
TILE7 = 7


def exchange_kernel(
    g_ref, r_ref, ent_ref, rel_ref,
    ring_ref, core_ref, acc_ref, hyp_ref, zb_ref, zr_ref, zf_ref, out_ref,
    ring_s, ring_r, core_s, core_r, hyp_s, hyp_r, zs_s, zs_r, za_s, za_r,
    ag_s, ag_r, last_s, last_r, a2a_s, a2a_r,
):
    p = lax.axis_index("pair")
    e = lax.axis_index("edge")
    core = p % 2
    chip = p // 2
    x = chip // 4
    y = chip % 4

    def at(xx, yy):
        return ((xx * 4 + yy) * 2 + core, e)

    partner = {
        "x1": at(x + 1 - 2 * (x % 2), y),
        "x2": at(3 - x, y),
        "y1": at(x, y + 1 - 2 * (y % 2)),
        "y2": at(x, 3 - y),
    }
    bit = {
        "x1": (x // 2 + x % 2) % 2,
        "x2": x // 2,
        "y1": (y // 2 + y % 2) % 2,
        "y2": y // 2,
    }
    order = [
        ("x1", "y1", "x2", "y2"),
        ("y1", "x2", "y2", "x1"),
        ("x2", "y2", "x1", "y1"),
        ("y2", "x1", "y1", "x2"),
    ]
    sibling = (p + 1 - 2 * core, e)

    barrier = pltpu.get_barrier_semaphore()
    for d in range(1, 32):
        pl.semaphore_signal(barrier, inc=1, device_id=((p + d) % 32, e), device_id_type=MESH)
    for d in range(1, 8):
        pl.semaphore_signal(barrier, inc=1, device_id=(p, (e + d) % 8), device_id_type=MESH)
    pl.semaphore_wait(barrier, 38)

    sent = []

    def push(src, dst, ss, rs, device):
        copy = pltpu.make_async_remote_copy(
            src_ref=src, dst_ref=dst, send_sem=ss, recv_sem=rs, device_id=device, device_id_type=MESH
        )
        copy.start()
        sent.append(copy)
        return copy

    streams = [(0, 0), (208, 1), (104, 0), (312, 1)]
    ring = {}

    def chunk(down, s):
        return (e + 1 + s) % 8 if down else (e + 7 - s) % 8

    def ring_send(s):
        for i, (row, down) in enumerate(streams):
            c = chunk(down, s)
            if s == 0:
                src = g_ref.at[c, pl.ds(row, RINGS)]
            else:
                ring[i].wait_recv()
                ring_ref[i, s - 1] += g_ref[c, pl.ds(row, RINGS), :]
                src = ring_ref.at[i, s - 1]
            to = (p, (e + 7) % 8) if down else (p, (e + 1) % 8)
            ring[i] = push(src, ring_ref.at[i, s], ring_s.at[i, s], ring_r.at[i, s], to)

    moves = {}
    off = [0, 0, 0, 0]
    offs = [[], [], [], []]
    base = [0, 8, 12, 14]

    def hyp_send(k, s):
        half = 8 >> s
        b = bit[order[k][s]]
        moves[k] = push(
            acc_ref.at[k, pl.ds(off[k] + (1 - b) * half, half)],
            hyp_ref.at[k, pl.ds(base[s], half)],
            hyp_s.at[k, s], hyp_r.at[k, s], partner[order[k][s]],
        )
        off[k] = off[k] + b * half
        offs[k].append(off[k])

    def hyp_take(k, s):
        half = 8 >> s
        moves[k].wait_recv()
        acc_ref[k, pl.ds(off[k], half)] += hyp_ref[k, pl.ds(base[s], half)]

    cores = [
        push(r_ref.at[1 - core, k], core_ref.at[k], core_s.at[k], core_r.at[k], sibling)
        for k in range(4)
    ]
    ring_send(0)
    for k in range(4):
        cores[k].wait_recv()
        acc_ref[k] = r_ref[core, k] + core_ref[k]
        hyp_send(k, 0)
    ring_send(1)

    def hyp_step(s):
        for k in range(4):
            hyp_take(k, s)
            if s < 3:
                hyp_send(k, s + 1)

    hyp_step(0)
    ring_send(2)
    hyp_step(1)
    hyp_step(2)
    ring_send(3)
    hyp_step(3)
    for t in range(TILE7):
        for k in range(4):
            zb_ref[t, k] = acc_ref[k, off[k], t]
    zb_ref[TILE7] = jnp.zeros((4, 8, 128), jnp.float32)
    zs = [
        push(zb_ref.at[(e + d) % 8], zr_ref.at[d], zs_s.at[d], zs_r.at[d], (p, (e + d) % 8))
        for d in range(1, 8)
    ]
    ring_send(4)
    total = zb_ref[e]
    for d in range(1, 8):
        zs[d - 1].wait_recv()
        total = total + zr_ref[d]
    zf_ref[e] = total
    za = [
        push(zf_ref.at[e], zf_ref.at[e], za_s.at[d], za_r.at[d], (p, (e + d) % 8))
        for d in range(1, 8)
    ]
    ring_send(5)
    for c in za:
        c.wait_recv()
    for t in range(TILE7):
        for k in range(4):
            rel_ref[core, k, off[k], t] = zf_ref[t, k]

    def gather_send(k, s):
        half = 8 >> s
        span = rel_ref.at[core, k, pl.ds(offs[k][s], half)]
        moves[k] = push(span, span, ag_s.at[k, s], ag_r.at[k, s], partner[order[k][s]])

    def gather_step(s):
        for k in range(4):
            moves[k].wait_recv()
            if s > 0:
                gather_send(k, s - 1)
            else:
                span = rel_ref.at[core, k]
                moves[k] = push(span, span, last_s.at[k], last_r.at[k], sibling)

    for k in range(4):
        gather_send(k, 3)
    gather_step(3)
    ring_send(6)
    gather_step(2)

    for half in range(2):
        parts = []
        for i, (row, down) in enumerate(streams):
            if down == half:
                ring[i].wait_recv()
                parts.append(ring_ref[i, 6] + g_ref[e, pl.ds(row, RINGS), :])
        full = jnp.concatenate(
            [parts[0][:HALF], parts[1][:HALF], jnp.zeros((56, CHUNK), jnp.float32)], axis=0
        ).T
        for n in range(32):
            out_ref[n, half] = full[n * 8:(n + 1) * 8, :]
    swap = [
        push(out_ref.at[(p + d) % 32], ent_ref.at[p], a2a_s.at[d], a2a_r.at[d], ((p + d) % 32, e))
        for d in range(1, 32)
    ]
    ent_ref[p] = out_ref[p]
    gather_step(1)
    gather_step(0)
    for c in swap:
        c.wait_recv()
    for k in range(4):
        moves[k].wait_recv()
    for c in sent:
        c.wait_send()


def exchange(g, r):
    vmem = pl.BlockSpec(memory_space=pltpu.VMEM)
    f32 = jnp.float32
    dma = pltpu.SemaphoreType.DMA
    return pl.pallas_call(
        exchange_kernel,
        out_shape=(
            jax.ShapeDtypeStruct((32, 2, 8, CHUNK), f32),
            jax.ShapeDtypeStruct((2, 4, 16, TILE7, 8, 128), f32),
        ),
        in_specs=[vmem] * 2,
        out_specs=(vmem, vmem),
        scratch_shapes=[
            pltpu.VMEM((4, 7, RINGS, CHUNK), f32),
            pltpu.VMEM((4, 16, TILE7, 8, 128), f32),
            pltpu.VMEM((4, 16, TILE7, 8, 128), f32),
            pltpu.VMEM((4, 15, TILE7, 8, 128), f32),
            pltpu.VMEM((8, 4, 8, 128), f32),
            pltpu.VMEM((8, 4, 8, 128), f32),
            pltpu.VMEM((8, 4, 8, 128), f32),
            pltpu.VMEM((32, 2, 8, CHUNK), f32),
            dma((4, 7)), dma((4, 7)), dma((4,)), dma((4,)), dma((4, 4)), dma((4, 4)),
            dma((8,)), dma((8,)), dma((8,)), dma((8,)),
            dma((4, 4)), dma((4, 4)), dma((4,)), dma((4,)), dma((32,)), dma((32,)),
        ],
        compiler_params=pltpu.CompilerParams(
            collective_id=0, has_side_effects=True, vmem_limit_bytes=48 * 1024 * 1024
        ),
        name="exchange",
    )(g, r)


def finish_kernel(plan_ref, ent_ref, rel_ref, out_ref, rel_out_ref):
    def put(i, c):
        out_ref[plan_ref[0, i]] = ent_ref[2 * i][:, :DIM]
        out_ref[plan_ref[1, i]] = ent_ref[2 * i + 1][:, :DIM]
        return c

    lax.fori_loop(0, 32, put, 0, unroll=4)

    def tile(n):
        v = rel_ref[pl.ds(n * 26, 26)].reshape(FEAT, 128)
        return jnp.concatenate([v[:HALF], v[HPAD:HPAD + HALF]], axis=0)

    def rows(n, c):
        rel_out_ref[:, pl.ds(pl.multiple_of(n * 128, 128), 128)] = tile(n)
        return c

    lax.fori_loop(0, 32, rows, 0, unroll=4)
    rel_out_ref[:, 4096:NREL] = tile(32)[:, :NREL - 4096]


def finish(plan, ent, rel):
    vmem = pl.BlockSpec(memory_space=pltpu.VMEM)
    return pl.pallas_call(
        finish_kernel,
        out_shape=(
            jax.ShapeDtypeStruct((64, 8, DIM), jnp.float32),
            jax.ShapeDtypeStruct((DIM, NREL), jnp.float32),
        ),
        in_specs=[pl.BlockSpec(memory_space=pltpu.SMEM), vmem, vmem],
        out_specs=(vmem, vmem),
        compiler_params=pltpu.CompilerParams(vmem_limit_bytes=32 * 1024 * 1024),
        name="finish",
    )(plan, ent, rel)


def local(entities, relations, edge_src, edge_rel, edge_dst, negatives, pair_live, pair_plan):
    plan = pair_plan.T
    tab, tn, xy, pos, tiles = fetch(plan, edge_rel, pair_live, entities, relations.T)
    ent, rel = edge_call(pair_live, pos, tiles, edge_src, edge_dst, negatives, edge_rel, tab, tn, xy)
    returned, rel_tiles = exchange(ent, rel.reshape(2, 4, 16, TILE7, 8, 128))
    ent_grad, rel_grad = finish(plan, returned.reshape(64, 8, CHUNK), rel_tiles.reshape(896, 8, 128))
    return ent_grad, rel_grad.T


def solution(mesh):
    placed = (
        P(None, ("pair", "edge"), None),
        P(),
        P("pair", "edge"),
        P("pair", "edge"),
        P("pair", "edge"),
        P("pair", "edge", None),
        P("pair"),
        P(),
    )
    return jax.shard_map(
        local,
        mesh=mesh,
        in_specs=placed,
        out_specs=(P(None, ("pair", "edge"), None), P()),
        check_vma=False,
    )
```

```python
import functools
import jax
import jax.numpy as jnp
from jax import lax
from jax.experimental import pallas as pl
from jax.experimental.pallas import tpu as pltpu
from jax.sharding import PartitionSpec as P

DIM = 200
HALF = 100
HPAD = 104
FEAT = 208
NREL = 4131
RTILE = 256
RTILES = 17
SPAN = 512
SPANS_DEV = 8
SLOTS = SPAN * SPANS_DEV
ROWS = 2048
CHUNK = 256
WIDE = 384
NN = (((1,), (0,)), ((), ()))
NT = (((1,), (1,)), ((), ()))
MESH = pl.DeviceIdType.MESH


def mm(a, b, dims=NN):
    return lax.dot_general(a, b, dims, preferred_element_type=jnp.float32)


def split2(v):
    hi = v.astype(jnp.bfloat16)
    lo = (v - hi.astype(jnp.float32)).astype(jnp.bfloat16)
    return jnp.concatenate([hi, lo], axis=0)


def place(ids):
    owner = ids // 64
    left = ids - owner * 64
    edge = left // 8
    return edge * 256 + owner * 8 + (left - edge * 8)


def edge_kernel(
    live_ref, pos_ref, tile_ref,
    src_ref, dst_ref, neg_ref, relid_ref, tab_ref, tn_ref, xy_ref,
    ent_ref, rel_ref,
    sc_ref, w_ref, ohs_ref, ohd_ref, ct_ref, perm_ref, sort_ref,
):
    live_here = live_ref[0] - lax.axis_index("edge") * SLOTS
    ent_ref[...] = jnp.zeros_like(ent_ref)
    s_ref = tab_ref.at[0]
    t_ref = tab_ref.at[1]

    def block(b, carry):
        at = pl.ds(pl.multiple_of(b * SPAN, SPAN), SPAN)
        src_row = place(src_ref[:, at])
        dst_row = place(dst_ref[:, at])
        neg_row = place(neg_ref[0, pl.ds(b, 1), :])
        for h in range(ROWS // CHUNK):
            ids = lax.broadcasted_iota(jnp.int32, (CHUNK, SPAN), 0) + h * CHUNK
            at = pl.ds(h * CHUNK, CHUNK)
            ohs_ref[at, :] = jnp.where(ids == src_row, 1.0, 0.0).astype(jnp.bfloat16)
            ohd_ref[at, :] = jnp.where(ids == dst_row, 1.0, 0.0).astype(jnp.bfloat16)
        neg_hi = neg_row // 128
        neg_lo = neg_row - neg_hi * 128
        oh_hi = jnp.where(lax.broadcasted_iota(jnp.int32, (16, 1024), 0) == neg_hi, 1.0, 0.0).astype(jnp.bfloat16)
        oh_lo = jnp.where(lax.broadcasted_iota(jnp.int32, (128, 1024), 0) == neg_lo, 1.0, 0.0).astype(jnp.bfloat16)
        counts = mm(oh_hi, oh_lo, NT)
        counts_t = mm(oh_lo, oh_hi, NT)
        for h in range(16):
            at = slice(h * 128, (h + 1) * 128)
            scaled = t_ref[:, at].astype(jnp.float32) * counts[h:h + 1, :]
            ct_ref[:, at] = split2(scaled)

        source = mm(s_ref[...], ohs_ref[...])
        target = mm(t_ref[...], ohd_ref[...])
        x = xy_ref[b, :HPAD]
        y = xy_ref[b, HPAD:]
        a, c = source[:HPAD], source[HPAD:]
        query_b = jnp.concatenate(
            [a * x - c * y, a * y + c * x, jnp.zeros((256 - FEAT, SPAN), jnp.float32)], axis=0
        ).astype(jnp.bfloat16)
        query = query_b[:FEAT].astype(jnp.float32)
        positive = jnp.sum(query * target, axis=0, keepdims=True)
        peak = positive
        for h in range(8):
            at = slice(h * CHUNK, (h + 1) * CHUNK)
            count = jnp.concatenate([counts_t[:, 2 * h:2 * h + 1], counts_t[:, 2 * h + 1:2 * h + 2]], axis=0)
            scores = mm(tn_ref[at, :], query_b)
            scores = jnp.where(count > 0.0, scores, -1e30)
            sc_ref[at, :] = scores
            peak = jnp.maximum(peak, jnp.max(scores, axis=0, keepdims=True))
        pos_exp = jnp.exp(positive - peak)
        total = pos_exp
        for h in range(8):
            at = slice(h * CHUNK, (h + 1) * CHUNK)
            count = jnp.concatenate([counts_t[:, 2 * h:2 * h + 1], counts_t[:, 2 * h + 1:2 * h + 2]], axis=0)
            e = jnp.exp(sc_ref[at, :] - peak)
            sc_ref[at, :] = e
            total = total + jnp.sum(e * count, axis=0, keepdims=True)
        inv = 1.0 / total
        live = jnp.where(
            lax.broadcasted_iota(jnp.int32, (1, SPAN), 1) + b * SPAN < live_here, 1.0, 0.0
        )
        coef = (pos_exp * inv - 1.0) * live
        inv = inv * live
        for h in range(8):
            at = slice(h * CHUNK, (h + 1) * CHUNK)
            w_ref[at, :] = (sc_ref[at, :] * inv).astype(jnp.bfloat16)
        both = mm(ct_ref[...], w_ref[...])
        grad_q = both[:FEAT] + both[FEAT:] + coef * target
        pos_q = split2(coef * query)
        g, k = grad_q[:HPAD], grad_q[HPAD:]
        grad_s = split2(jnp.concatenate([g * x + k * y, k * x - g * y], axis=0))
        relrow = relid_ref[:, pl.ds(pl.multiple_of(b * SPAN, SPAN), SPAN)].astype(jnp.float32)
        first = lax.broadcasted_iota(jnp.int32, (24, SPAN), 0) == 0
        perm_ref[:, 0, :] = jnp.concatenate(
            [g * a + k * c, jnp.where(first, relrow, 0.0)], axis=0
        ).T
        perm_ref[:, 1, :] = jnp.concatenate(
            [k * a - g * c, jnp.zeros((24, SPAN), jnp.float32)], axis=0
        ).T

        for h in range(8):
            at = slice(h * CHUNK, (h + 1) * CHUNK)
            oh = ohs_ref[at, :]
            for j in range(h * 64, h * 64 + 64):
                sort_ref[pos_ref[b * SPAN + j]] = perm_ref[j]
            back = mm(grad_s, oh, NT)
            ent_ref[h, :FEAT, :] += back[:FEAT] + back[FEAT:]
            neg = mm(query_b[:FEAT], w_ref[at, :], NT)
            pos = mm(pos_q, ohd_ref[at, :], NT)
            count = jnp.concatenate([counts[2 * h:2 * h + 1, :], counts[2 * h + 1:2 * h + 2, :]], axis=1)
            ent_ref[h, FEAT:, :] += neg * count + (pos[:FEAT] + pos[FEAT:])
        return carry

    lax.fori_loop(0, live_blocks_of(live_here), block, 0)

    def piece(t, n):
        left = tile_ref[t, 1] - n * WIDE
        base = tile_ref[t, 0] + n * WIDE
        ok = lax.broadcasted_iota(jnp.int32, (WIDE, 128), 0) < left
        re = jnp.where(ok, sort_ref[pl.ds(base, WIDE), 0, :], 0.0).T
        im = jnp.where(ok, sort_ref[pl.ds(base, WIDE), 1, :], 0.0).T
        names = re[HPAD:HPAD + 1, :].astype(jnp.int32)
        oh = jnp.where(
            lax.broadcasted_iota(jnp.int32, (RTILE, WIDE), 0) + t * RTILE == names, 1.0, 0.0
        ).astype(jnp.bfloat16)
        part = mm(split2(jnp.concatenate([re[:HPAD], im[:HPAD]], axis=0)), oh, NT)
        part = part[:FEAT] + part[FEAT:]
        return part[:, :128].reshape(26, 8, 128), part[:, 128:].reshape(26, 8, 128)

    for t in range(RTILES):
        one, two = piece(t, 0)
        rel_ref[52 * t:52 * t + 26] = one
        rel_ref[52 * t + 26:52 * t + 52] = two

    def tile(t, carry):
        def more(n, c):
            one, two = piece(t, n)
            rel_ref[pl.ds(52 * t, 26)] += one
            rel_ref[pl.ds(52 * t + 26, 26)] += two
            return c

        return lax.fori_loop(1, (tile_ref[t, 1] + WIDE - 1) // WIDE, more, carry)

    lax.fori_loop(0, RTILES, tile, 0)
    rel_ref[884:] = jnp.zeros((12, 8, 128), jnp.float32)


def edge_call(live, pos, tiles, src, dst, neg, relid, tab, tn, xy):
    smem = pl.BlockSpec(memory_space=pltpu.SMEM)
    vmem = pl.BlockSpec(memory_space=pltpu.VMEM)
    return pl.pallas_call(
        edge_kernel,
        out_shape=(
            jax.ShapeDtypeStruct((8, 2 * FEAT, CHUNK), jnp.float32),
            jax.ShapeDtypeStruct((896, 8, 128), jnp.float32),
        ),
        in_specs=[smem] * 3 + [vmem] * 7,
        out_specs=(vmem, vmem),
        scratch_shapes=[
            pltpu.VMEM((ROWS, SPAN), jnp.float32),
            pltpu.VMEM((ROWS, SPAN), jnp.bfloat16),
            pltpu.VMEM((ROWS, SPAN), jnp.bfloat16),
            pltpu.VMEM((ROWS, SPAN), jnp.bfloat16),
            pltpu.VMEM((2 * FEAT, ROWS), jnp.bfloat16),
            pltpu.VMEM((SPAN, 2, 128), jnp.float32),
            pltpu.VMEM((SLOTS + WIDE, 2, 128), jnp.float32),
        ],
        compiler_params=pltpu.CompilerParams(vmem_limit_bytes=56 * 1024 * 1024),
        name="edges",
    )(live, pos, tiles, src, dst, neg, relid, tab, tn, xy)


def fetch_kernel(
    plan_ref, relid_ref, live_ref, relrow_ref, ent_ref, rel_hbm,
    tab_ref, tn_ref, xy_ref, pos_ref, tile_ref,
    relt_ref, table_ref, rows_ref, stage_ref, got_ref, ag_ref,
    rel_sem, a2a_s, a2a_r, ag_s, ag_r,
):
    p = lax.axis_index("pair")
    e = lax.axis_index("edge")
    load = pltpu.make_async_copy(rel_hbm, relt_ref, rel_sem)
    load.start()
    barrier = pltpu.get_barrier_semaphore()
    for d in range(1, 32):
        pl.semaphore_signal(barrier, inc=1, device_id=((p + d) % 32, e), device_id_type=MESH)
    for d in (1, 7):
        pl.semaphore_signal(barrier, inc=1, device_id=(p, (e + d) % 8), device_id_type=MESH)

    gap = jnp.zeros((16, 256 - DIM), jnp.float32)

    def stage(n, c):
        both = jnp.concatenate(
            [ent_ref[plan_ref[0, n]].astype(jnp.float32), ent_ref[plan_ref[1, n]].astype(jnp.float32)], axis=0
        )
        stage_ref[n] = jnp.concatenate([both, gap], axis=1).astype(jnp.bfloat16)
        return c

    lax.fori_loop(0, 32, stage, 0, unroll=4)
    pl.semaphore_wait(barrier, 33)
    sent = []

    def push(src, dst, ss, rs, device):
        copy = pltpu.make_async_remote_copy(
            src_ref=src, dst_ref=dst, send_sem=ss, recv_sem=rs, device_id=device, device_id_type=MESH
        )
        copy.start()
        sent.append(copy)
        return copy

    swap = [
        push(stage_ref.at[(p + d) % 32], got_ref.at[p], a2a_s.at[d], a2a_r.at[d], ((p + d) % 32, e))
        for d in range(1, 32)
    ]
    got_ref[p] = stage_ref[p]

    valid = live_blocks_of(live_ref[0] - e * SLOTS) * SPAN
    ones = []
    total = jnp.zeros((32, 1), jnp.float32)
    sub = lax.broadcasted_iota(jnp.int32, (32, 128), 0)
    lane = lax.broadcasted_iota(jnp.int32, (32, 128), 1)
    for c in range(32):
        which = relrow_ref[:, c * 128:(c + 1) * 128] // RTILE
        one = jnp.where((sub == which) & (lane + c * 128 < valid), 1.0, 0.0)
        size = jnp.sum(one, axis=1, keepdims=True)
        ones.append((one, size))
        total = total + size
    below = jnp.where(
        lax.broadcasted_iota(jnp.int32, (32, 32), 1) < lax.broadcasted_iota(jnp.int32, (32, 32), 0), 1.0, 0.0
    )
    begin = lax.dot_general(
        below, jnp.broadcast_to(total, (32, 128)), NN,
        precision=lax.Precision.HIGHEST, preferred_element_type=jnp.float32,
    )
    tile_ref[...] = jnp.where(lane == 0, begin, total).astype(jnp.int32)
    ahead = jnp.where(
        lax.broadcasted_iota(jnp.int32, (128, 128), 0) < lax.broadcasted_iota(jnp.int32, (128, 128), 1), 1.0, 0.0
    ).astype(jnp.bfloat16)
    for c in range(32):
        one, size = ones[c]
        place = one * (mm(one.astype(jnp.bfloat16), ahead) + begin)
        pos_ref[c:c + 1, :] = jnp.sum(place, axis=0, keepdims=True).astype(jnp.int32)
        begin = begin + size

    load.wait()

    def turn(n, v):
        v = jnp.concatenate([v, jnp.zeros((28, 128), jnp.float32)], axis=0)
        w = jnp.concatenate([v[HALF:DIM], jnp.zeros((28, 128), jnp.float32)], axis=0)
        table_ref[pl.ds(n * 128, 128), 0, :] = v[:128].T
        table_ref[pl.ds(n * 128, 128), 1, :] = w.T

    def build(n, c):
        turn(n, relt_ref[:, pl.ds(pl.multiple_of(n * 128, 128), 128)])
        return c

    lax.fori_loop(0, 32, build, 0, unroll=4)
    tail = jnp.concatenate([relt_ref[:, 4096:NREL], jnp.zeros((DIM, 4224 - NREL), jnp.float32)], axis=1)
    turn(32, tail)

    for c in swap:
        c.wait_recv()
    for s in range(2):
        rows = got_ref[...].astype(jnp.float32)[:, s * 8:(s + 1) * 8, :].reshape(CHUNK, 256)
        cols = rows.T
        zero = jnp.zeros((HPAD - HALF, CHUNK), jnp.float32)
        ag_ref[e, s] = jnp.concatenate([cols[:HALF], zero, cols[HALF:DIM], zero], axis=0).astype(jnp.bfloat16)

    hops = {}

    def forward(h, way, s):
        o = (e + 8 - (h - 1)) % 8 if way == 0 else (e + (h - 1)) % 8
        to = (p, (e + 1) % 8) if way == 0 else (p, (e + 7) % 8)
        hops[way, s] = push(
            ag_ref.at[o, s], ag_ref.at[o, s], ag_s.at[way, s, h - 1], ag_r.at[way, s, h - 1], to
        )

    def settle(o):
        at = pl.ds(pl.multiple_of(o * CHUNK, CHUNK), CHUNK)
        tab_ref[0, :, at] = ag_ref[o, 0]
        tab_ref[1, :, at] = ag_ref[o, 1]
        part = ag_ref[o, 1].astype(jnp.float32)
        part = jnp.concatenate([part, jnp.zeros((256 - FEAT, CHUNK), jnp.float32)], axis=0)
        tn_ref[at, :] = part.T.astype(jnp.bfloat16)

    def relations_of(b):
        def fetch_row(j, c):
            rows_ref[j] = table_ref[relid_ref[0, b * SPAN + j]]
            return c

        lax.fori_loop(0, SPAN, fetch_row, 0, unroll=16)
        xy_ref[b, :HPAD] = jnp.where(keep, rows_ref[:, 0, :].T[:HPAD], 0.0)
        xy_ref[b, HPAD:] = rows_ref[:, 1, :].T[:HPAD]

    keep = lax.broadcasted_iota(jnp.int32, (HPAD, SPAN), 0) < HALF
    all_streams = [(0, 0), (1, 1), (0, 1), (1, 0)]
    for way, s in all_streams:
        forward(1, way, s)
    settle(e)
    relations_of(0)
    relations_of(1)
    for h in range(1, 4):
        for way, s in all_streams:
            hops[way, s].wait_recv()
            if h < 3 or way == s:
                forward(h + 1, way, s)
        settle((e + 8 - h) % 8)
        settle((e + h) % 8)
        relations_of(2 * h)
        relations_of(2 * h + 1)
    hops[0, 0].wait_recv()
    hops[1, 1].wait_recv()
    settle((e + 4) % 8)
    for c in sent:
        c.wait_send()


def live_blocks_of(live_here):
    return jnp.clip((live_here + SPAN - 1) // SPAN, 0, SPANS_DEV)


def fetch(plan, relid, live, entities, relations_t):
    smem = pl.BlockSpec(memory_space=pltpu.SMEM)
    vmem = pl.BlockSpec(memory_space=pltpu.VMEM)
    f32 = jnp.float32
    bf16 = jnp.bfloat16
    dma = pltpu.SemaphoreType.DMA
    return pl.pallas_call(
        fetch_kernel,
        out_shape=(
            jax.ShapeDtypeStruct((2, FEAT, ROWS), bf16),
            jax.ShapeDtypeStruct((ROWS, 256), bf16),
            jax.ShapeDtypeStruct((SPANS_DEV, FEAT, SPAN), f32),
            jax.ShapeDtypeStruct((32, 128), jnp.int32),
            jax.ShapeDtypeStruct((32, 128), jnp.int32),
        ),
        in_specs=[smem, smem, smem, vmem, vmem, pl.BlockSpec(memory_space=pl.ANY)],
        out_specs=(vmem,) * 5,
        scratch_shapes=[
            pltpu.VMEM((DIM, NREL), f32),
            pltpu.VMEM((4224, 2, 128), f32),
            pltpu.VMEM((SPAN, 2, 128), f32),
            pltpu.VMEM((32, 16, 256), bf16),
            pltpu.VMEM((32, 16, 256), bf16),
            pltpu.VMEM((8, 2, FEAT, CHUNK), bf16),
            dma, dma((32,)), dma((32,)), dma((2, 2, 4)), dma((2, 2, 4)),
        ],
        compiler_params=pltpu.CompilerParams(
            collective_id=1, has_side_effects=True, vmem_limit_bytes=56 * 1024 * 1024
        ),
        name="fetch",
    )(plan, relid, live, relid, entities, relations_t)


RINGS = 104
TILE7 = 7


def exchange_kernel(
    g_hbm, r_hbm, ent_ref, rel_ref,
    g_ref, r_ref, load_s,
    ring_ref, core_ref, acc_ref, hyp_ref, zb_ref, zr_ref, zf_ref, out_ref,
    ring_s, ring_r, core_s, core_r, hyp_s, hyp_r, zs_s, zs_r, za_s, za_r,
    ag_s, ag_r, last_s, last_r, a2a_s, a2a_r,
):
    p = lax.axis_index("pair")
    e = lax.axis_index("edge")
    core = p % 2
    chip = p // 2
    x = chip // 4
    y = chip % 4

    def at(xx, yy):
        return ((xx * 4 + yy) * 2 + core, e)

    partner = {
        "x1": at(x + 1 - 2 * (x % 2), y),
        "x2": at(3 - x, y),
        "y1": at(x, y + 1 - 2 * (y % 2)),
        "y2": at(x, 3 - y),
    }
    bit = {
        "x1": (x // 2 + x % 2) % 2,
        "x2": x // 2,
        "y1": (y // 2 + y % 2) % 2,
        "y2": y // 2,
    }
    order = [
        ("x1", "y1", "x2", "y2"),
        ("y1", "x2", "y2", "x1"),
        ("x2", "y2", "x1", "y1"),
        ("y2", "x1", "y1", "x2"),
    ]
    sibling = (p + 1 - 2 * core, e)
    load_r = pltpu.make_async_copy(r_hbm.at[core], r_ref, load_s.at[0])
    load_r.start()
    load_g = pltpu.make_async_copy(g_hbm, g_ref, load_s.at[1])
    load_g.start()

    barrier = pltpu.get_barrier_semaphore()
    for d in range(1, 32):
        pl.semaphore_signal(barrier, inc=1, device_id=((p + d) % 32, e), device_id_type=MESH)
    for d in range(1, 8):
        pl.semaphore_signal(barrier, inc=1, device_id=(p, (e + d) % 8), device_id_type=MESH)
    pl.semaphore_wait(barrier, 38)

    sent = []

    def push(src, dst, ss, rs, device):
        copy = pltpu.make_async_remote_copy(
            src_ref=src, dst_ref=dst, send_sem=ss, recv_sem=rs, device_id=device, device_id_type=MESH
        )
        copy.start()
        sent.append(copy)
        return copy

    streams = [(0, 0), (208, 1), (104, 0), (312, 1)]
    ring = {}

    def chunk(down, s):
        return (e + 1 + s) % 8 if down else (e + 7 - s) % 8

    def ring_send(s):
        for i, (row, down) in enumerate(streams):
            c = chunk(down, s)
            if s == 0:
                src = g_hbm.at[c, pl.ds(row, RINGS)]
            else:
                ring[i].wait_recv()
                ring_ref[i, s - 1] += g_ref[c, pl.ds(row, RINGS), :]
                src = ring_ref.at[i, s - 1]
            to = (p, (e + 7) % 8) if down else (p, (e + 1) % 8)
            ring[i] = push(src, ring_ref.at[i, s], ring_s.at[i, s], ring_r.at[i, s], to)

    moves = {}
    off = {(k, q): 0 for k in range(4) for q in range(2)}
    offs = {(k, q): [] for k in range(4) for q in range(2)}
    base = [0, 8, 12, 14]

    chains = [(k, q) for q in range(2) for k in range(4)]
    cut = [pl.ds(0, 4), pl.ds(4, 3)]

    def hyp_send(k, q, s):
        half = 8 >> s
        b = bit[order[k][s]]
        moves[k, q] = push(
            acc_ref.at[k, pl.ds(off[k, q] + (1 - b) * half, half), cut[q]],
            hyp_ref.at[k, pl.ds(base[s], half), cut[q]],
            hyp_s.at[k, q, s], hyp_r.at[k, q, s], partner[order[k][s]],
        )
        off[k, q] = off[k, q] + b * half
        offs[k, q].append(off[k, q])

    def hyp_take(k, q, s):
        half = 8 >> s
        moves[k, q].wait_recv()
        at = (k, pl.ds(off[k, q], half), cut[q])
        acc_ref[at] += hyp_ref[k, pl.ds(base[s], half), cut[q]]

    cores = {
        (k, q): push(
            r_hbm.at[1 - core, k, :, cut[q]], core_ref.at[k, :, cut[q]],
            core_s.at[k, q], core_r.at[k, q], sibling,
        )
        for k, q in chains
    }
    ring_send(0)
    load_r.wait()
    for k, q in chains:
        cores[k, q].wait_recv()
        acc_ref[k, :, cut[q]] = r_ref[k, :, cut[q]] + core_ref[k, :, cut[q]]
        hyp_send(k, q, 0)
    load_g.wait()
    ring_send(1)

    def hyp_step(s):
        for k, q in chains:
            hyp_take(k, q, s)
            if s < 3:
                hyp_send(k, q, s + 1)

    hyp_step(0)
    ring_send(2)
    hyp_step(1)
    hyp_step(2)
    ring_send(3)
    tiles = [[(t, k) for t in range(4) for k in range(4)], [(t, k) for t in range(4, 7) for k in range(4)]]
    zmoves = [None, None]
    zb_ref[1, 6:] = jnp.zeros((2, 2, 8, 128), jnp.float32)

    def z_send(q):
        for k in range(4):
            hyp_take(k, q, 3)
        for i, (t, k) in enumerate(tiles[q]):
            zb_ref[q, i // 2, i % 2] = acc_ref[k, off[k, q], t]
        zmoves[q] = [
            push(
                zb_ref.at[q, (e + d) % 8], zr_ref.at[q, d], zs_s.at[q, d], zs_r.at[q, d], (p, (e + d) % 8)
            )
            for d in range(1, 8)
        ]

    def z_sum(q):
        total = zb_ref[q, e]
        for d in range(1, 8):
            zmoves[q][d - 1].wait_recv()
            total = total + zr_ref[q, d]
        zf_ref[q, e] = total
        zmoves[q] = [
            push(zf_ref.at[q, e], zf_ref.at[q, e], za_s.at[q, d], za_r.at[q, d], (p, (e + d) % 8))
            for d in range(1, 8)
        ]

    def z_spread(q):
        for c in zmoves[q]:
            c.wait_recv()
        for i, (t, k) in enumerate(tiles[q]):
            rel_ref[core, k, off[k, q], t] = zf_ref[q, i // 2, i % 2]
        for k in range(4):
            gather_send(k, q, 3)

    def gather_send(k, q, s):
        half = 8 >> s
        span = rel_ref.at[core, k, pl.ds(offs[k, q][s], half), cut[q]]
        moves[k, q] = push(span, span, ag_s.at[k, q, s], ag_r.at[k, q, s], partner[order[k][s]])

    def gather_step(s):
        for k, q in chains:
            moves[k, q].wait_recv()
            if s > 0:
                gather_send(k, q, s - 1)
            else:
                span = rel_ref.at[core, k, :, cut[q]]
                moves[k, q] = push(span, span, last_s.at[k, q], last_r.at[k, q], sibling)

    z_send(0)
    z_send(1)
    ring_send(4)
    z_sum(0)
    z_sum(1)
    z_spread(0)
    z_spread(1)
    ring_send(5)
    gather_step(3)
    gather_step(2)
    ring_send(6)
    gather_step(1)

    for half in range(2):
        parts = []
        for i, (row, down) in enumerate(streams):
            if down == half:
                ring[i].wait_recv()
                parts.append(ring_ref[i, 6] + g_ref[e, pl.ds(row, RINGS), :])
        full = jnp.concatenate(
            [parts[0][:HALF], parts[1][:HALF], jnp.zeros((56, CHUNK), jnp.float32)], axis=0
        ).T
        for n in range(32):
            out_ref[n, half] = full[n * 8:(n + 1) * 8, :]
    swap = [
        push(out_ref.at[(p + d) % 32], ent_ref.at[p], a2a_s.at[d], a2a_r.at[d], ((p + d) % 32, e))
        for d in range(1, 32)
    ]
    ent_ref[p] = out_ref[p]
    gather_step(0)
    for c in swap:
        c.wait_recv()
    for k, q in chains:
        moves[k, q].wait_recv()
    for c in sent:
        c.wait_send()


def exchange(g, r):
    vmem = pl.BlockSpec(memory_space=pltpu.VMEM)
    f32 = jnp.float32
    dma = pltpu.SemaphoreType.DMA
    return pl.pallas_call(
        exchange_kernel,
        out_shape=(
            jax.ShapeDtypeStruct((32, 2, 8, CHUNK), f32),
            jax.ShapeDtypeStruct((2, 4, 16, TILE7, 8, 128), f32),
        ),
        in_specs=[pl.BlockSpec(memory_space=pl.ANY)] * 2,
        out_specs=(vmem, vmem),
        scratch_shapes=[
            pltpu.VMEM((8, 2 * FEAT, CHUNK), f32),
            pltpu.VMEM((4, 16, TILE7, 8, 128), f32),
            dma((2,)),
            pltpu.VMEM((4, 7, RINGS, CHUNK), f32),
            pltpu.VMEM((4, 16, TILE7, 8, 128), f32),
            pltpu.VMEM((4, 16, TILE7, 8, 128), f32),
            pltpu.VMEM((4, 15, TILE7, 8, 128), f32),
            pltpu.VMEM((2, 8, 2, 8, 128), f32),
            pltpu.VMEM((2, 8, 2, 8, 128), f32),
            pltpu.VMEM((2, 8, 2, 8, 128), f32),
            pltpu.VMEM((32, 2, 8, CHUNK), f32),
            dma((4, 7)), dma((4, 7)), dma((4, 2)), dma((4, 2)), dma((4, 2, 4)), dma((4, 2, 4)),
            dma((2, 8)), dma((2, 8)), dma((2, 8)), dma((2, 8)),
            dma((4, 2, 4)), dma((4, 2, 4)), dma((4, 2)), dma((4, 2)), dma((32,)), dma((32,)),
        ],
        compiler_params=pltpu.CompilerParams(
            collective_id=0, has_side_effects=True, vmem_limit_bytes=56 * 1024 * 1024
        ),
        name="exchange",
    )(g, r)


def finish_kernel(plan_ref, ent_ref, rel_ref, out_ref, rel_out_ref):
    def put(i, c):
        out_ref[plan_ref[0, i]] = ent_ref[2 * i][:, :DIM]
        out_ref[plan_ref[1, i]] = ent_ref[2 * i + 1][:, :DIM]
        return c

    lax.fori_loop(0, 32, put, 0, unroll=4)

    def tile(n):
        v = rel_ref[pl.ds(n * 26, 26)].reshape(FEAT, 128)
        return jnp.concatenate([v[:HALF], v[HPAD:HPAD + HALF]], axis=0)

    def rows(n, c):
        rel_out_ref[:, pl.ds(pl.multiple_of(n * 128, 128), 128)] = tile(n)
        return c

    lax.fori_loop(0, 32, rows, 0, unroll=4)
    rel_out_ref[:, 4096:NREL] = tile(32)[:, :NREL - 4096]


def finish(plan, ent, rel):
    vmem = pl.BlockSpec(memory_space=pltpu.VMEM)
    return pl.pallas_call(
        finish_kernel,
        out_shape=(
            jax.ShapeDtypeStruct((64, 8, DIM), jnp.float32),
            jax.ShapeDtypeStruct((DIM, NREL), jnp.float32),
        ),
        in_specs=[pl.BlockSpec(memory_space=pltpu.SMEM), vmem, vmem],
        out_specs=(vmem, vmem),
        compiler_params=pltpu.CompilerParams(vmem_limit_bytes=32 * 1024 * 1024),
        name="finish",
    )(plan, ent, rel)


def local(entities, relations, edge_src, edge_rel, edge_dst, negatives, pair_live, pair_plan):
    plan = pair_plan.T
    tab, tn, xy, pos, tiles = fetch(plan, edge_rel, pair_live, entities, relations.T)
    ent, rel = edge_call(pair_live, pos.reshape(SLOTS), tiles, edge_src, edge_dst, negatives, edge_rel, tab, tn, xy)
    returned, rel_tiles = exchange(ent, rel.reshape(2, 4, 16, TILE7, 8, 128))
    ent_grad, rel_grad = finish(plan, returned.reshape(64, 8, CHUNK), rel_tiles.reshape(896, 8, 128))
    return ent_grad, rel_grad.T


def solution(mesh):
    placed = (
        P(None, ("pair", "edge"), None),
        P(),
        P("pair", "edge"),
        P("pair", "edge"),
        P("pair", "edge"),
        P("pair", "edge", None),
        P("pair"),
        P(),
    )
    return jax.shard_map(
        local,
        mesh=mesh,
        in_specs=placed,
        out_specs=(P(None, ("pair", "edge"), None), P()),
        check_vma=False,
    )
```
